512 devices in a mesh: pipe: 16 (over z), dp: 8 (over y, x_hi), tensor: 4 (over x_lo, core).
Axes of the slice: x: 4 (x_hi: 2, x_lo: 2; x = x_hi * 2 + x_lo), y: 4, z: 16, core: 2. Of those that a mesh axis runs over, the one named last changes fastest.
Arguments:
- inputs: bfloat16 [2, 8, 64, 7168], P(None, 'dp', None, 'tensor'), may hold values from -6 to 6
- lengths: int32 [2, 8, 4], P(None, 'dp'), may hold values from 1 to 32, 64 in all within a row
- w_down: bfloat16 [16, 7168, 512], P('pipe', 'tensor', 'dp'), may hold values from -0.0625 to 0.0625
- w_query: bfloat16 [16, 512, 512], P('pipe', 'dp', 'tensor'), may hold values from -0.25 to 0.25
- w_out: bfloat16 [16, 512, 7168], P('pipe', 'dp', 'tensor'), may hold values from -0.25 to 0.25
- gain_latent: bfloat16 [16, 512], P('pipe'), may hold values from 0.25 to 1.75
- readout: bfloat16 [7168], P('tensor'), may hold values from -0.0625 to 0.0625
Outputs:
- latents: bfloat16 [16, 2, 8, 64, 512], P('pipe', None, 'dp')
- scores: float32 [2, 8, 64], P(None, 'dp')
The draws below stay inside these ranges and needn't reach their ends.
Inputs may be any that keep to these rules, and one draw needn't show every extreme that they name: Each micro-batch's lengths sum to 64; the longest is exactly 32.
All inputs are finite; a program needn't handle non-finite values.
Results may differ from the reference program's by a relative error of at most 0.035.
Values may be sent and summed in bfloat16 or wider, within the bound.
A program may use at most 64 MiB of HBM per device.

```python
import math
import jax
import jax.numpy as jnp
import numpy as np
from jax import lax

D = 7168
KR = 512
SEQ = 64
DOCS = 4
LAYERS = 16
BATCH = 8


def block_levels(stream_key, dims, cuts, low, largest):
    def one(position, shards_of):
        heights = jax.random.uniform(jax.random.fold_in(jax.random.fold_in(stream_key, 6), position), (shards_of,), jnp.float32, low / len(cuts), largest / len(cuts))
        return jnp.repeat(jnp.exp(heights), dims[position] // shards_of).reshape((-1,) + (1,) * (len(dims) - position - 1))

    level = one(*cuts[0])
    for cut in cuts[1:]:
        level = level * one(*cut)
    return level


def split_up(number_of, total, most, skew):
    portions = [(1 << 20) // math.isqrt(rank ** skew) + 1 for rank in range(2, number_of + 1)]
    spare, given = total - most - (number_of - 1), [1] * (number_of - 1)
    while spare > 0:
        movable = [i for i in range(number_of - 1) if given[i] < most]
        whole, budget = sum([portions[i] for i in movable]), spare
        for i in movable:
            more = min(most - given[i], max(1, budget * portions[i] // whole), spare)
            given[i] = given[i] + more
            spare = spare - more
    return np.array([most] + given)


def ragged_sizes(key, amount, total, bound, skew):
    if amount == 2:
        one = jax.random.randint(key, (), max(1, total - bound), min(bound, total - 1) + 1)
        return jnp.stack([one, total - one])
    sizes = jnp.asarray(split_up(amount, total, bound, skew), jnp.int32)
    twos = (amount - 1) // 2
    donor, receiver = sizes[1:1 + 2 * twos:2], sizes[2:2 + 2 * twos:2]
    slack = jnp.minimum(donor - 1, bound - receiver)
    passed = jax.random.randint(jax.random.fold_in(key, 1), (twos,), 0, 1 << 20) % (slack + 1)
    sizes = sizes.at[1:1 + 2 * twos:2].set(donor - passed).at[2:2 + 2 * twos:2].set(receiver + passed)
    return sizes[jax.random.permutation(jax.random.fold_in(key, 2), amount)]


def gaussian(stream_key, shape, width, limit, shards=(), dtype=jnp.bfloat16):
    level = block_levels(stream_key, shape, shards, -0.22, 0.18) if shards else 1.0
    array = jax.random.normal(stream_key, shape, jnp.float32) * width * level
    return jnp.minimum(jnp.maximum(array, -limit), limit).astype(dtype)


def setup_inputs(seed: int = 0) -> dict:
    key_list = jax.random.split(jax.random.key(seed), 8)
    return {
        "inputs": gaussian(key_list[0], (2, BATCH, SEQ, D), 1.0, 6.0, ((1, 8), (3, 4))),
        "lengths": jax.vmap(lambda own: ragged_sizes(own, DOCS, SEQ, SEQ // 2, 0))(jax.random.split(key_list[1], 2 * BATCH)).reshape((2, BATCH, DOCS)).astype(jnp.int32),
        "w_down": gaussian(key_list[2], (LAYERS, D, KR), D ** -0.5, 0.0625, ((0, 16), (1, 4), (2, 8))),
        "w_query": gaussian(key_list[3], (LAYERS, KR, KR), KR ** -0.5, 0.25, ((0, 16), (1, 8), (2, 4))),
        "w_out": gaussian(key_list[4], (LAYERS, KR, D), KR ** -0.5, 0.25, ((0, 16), (1, 8), (2, 4))),
        "gain_latent": jnp.clip(1.0 + 0.15 * jax.random.normal(key_list[5], (LAYERS, KR), jnp.float32), 0.25, 1.75).astype(jnp.bfloat16),
        "readout": gaussian(key_list[6], (D,), D ** -0.5, 0.0625, ((0, 4),)),
    }


def doc_mask(row_lengths, seq):
    ends = jnp.cumsum(row_lengths)
    positions = jnp.arange(seq)
    doc = lax.optimization_barrier(jnp.sum((positions[:, None] >= ends[None, :]).astype(jnp.int32), axis=1))
    return (doc[:, None] == doc[None, :]) & (positions[None, :] <= positions[:, None])

def one_layer(hidden, mask, down, query_map, out_map, gain):
    part = jnp.dot(hidden, down, preferred_element_type=jnp.float32)
    scale = lax.rsqrt(lax.optimization_barrier(jnp.mean(part * part, axis=1, keepdims=True)) + 1e-06)
    latent = (part * scale * gain.astype(jnp.float32)).astype(jnp.bfloat16)
    query = jnp.dot(latent, query_map, preferred_element_type=jnp.float32).astype(jnp.bfloat16)
    logits = jnp.dot(query, latent.T, preferred_element_type=jnp.float32) / jnp.sqrt(jnp.float32(latent.shape[1]))
    logits = jnp.where(mask, logits, jnp.float32(-1e+30))
    weights = jax.nn.softmax(logits, axis=1).astype(jnp.bfloat16)
    mixed = jnp.dot(weights, latent, preferred_element_type=jnp.float32).astype(jnp.bfloat16)
    update = jnp.dot(mixed, out_map, preferred_element_type=jnp.float32)
    return ((hidden.astype(jnp.float32) + update).astype(jnp.bfloat16), latent)

def reference(inputs, lengths, w_down, w_query, w_out, gain_latent, readout):
    flat = inputs.reshape((2 * BATCH, SEQ, D))
    masks = jax.vmap(lambda row: doc_mask(row, SEQ))(lengths.reshape((2 * BATCH, DOCS)))

    def layer_step(hidden_all, weights):
        down, query_map, out_map, gain = weights

        def per_batch(pair):
            return one_layer(pair[0], pair[1], down, query_map, out_map, gain)
        new_hidden, latent = lax.map(per_batch, (hidden_all, masks))
        return (new_hidden, latent)
    final, kept = lax.scan(layer_step, flat, (w_down, w_query, w_out, gain_latent))
    kept = kept.reshape((LAYERS, 2, BATCH, SEQ, KR))
    latents = jnp.stack([kept[:, 0], kept[::-1, 1]], axis=1)
    scores = lax.optimization_barrier(jnp.sum(final.astype(jnp.float32) * readout.astype(jnp.float32)[None, None, :], axis=2))
    return (latents, scores.reshape((2, BATCH, SEQ)))
```

```python
import functools

import jax
import jax.numpy as jnp
from jax import lax
from jax.experimental import pallas as pl
from jax.experimental.pallas import tpu as pltpu
from jax.sharding import PartitionSpec as P

F32 = jnp.float32
BF16 = jnp.bfloat16
MESH = pl.DeviceIdType.MESH


def nt_dot(a, b):
    return lax.dot_general(a, b, (((1,), (1,)), ((), ())), preferred_element_type=F32)


def dot(a, b):
    return jnp.dot(a, b, preferred_element_type=F32)


def kernel(
    n, nd,
    x_hbm, len_ref, wd_hbm, wq_hbm, wo_hbm, gain_ref, read_ref,
    lat_out, score_out,
    xv, wd, wq, ring, csend, crecv, g, gnear, p0send, p0recv, acc, p2, near2,
    mixed, latv, lat, sin, sout, fin, maskv, dummy,
    loc, asem, qsem, ups, upr, dns, dnr, cs, cr, d1s, d1r, d2s, d2r,
    nx, psem, ms, mr, ex, ssem, lats, latr, fs, fr,
):
    seq = latv.shape[0]
    width = latv.shape[1]
    half = width // 2
    rows = wo_hbm.shape[0]
    quarter = wq_hbm.shape[1]
    ny = nd // 2
    up_steps = n // 2
    low = up_steps - 2
    last = n - 1

    l = lax.axis_index("pipe")
    d = lax.axis_index("dp")
    t = lax.axis_index("tensor")
    y, xh = d // 2, d % 2
    e, c = t // 2, t % 2

    def tensor_of(x_low, core):
        return 2 * x_low + core

    gather_peers = [(l, (d + k) % nd, t) for k in range(1, nd)]
    cut_peers = [(e, 1 - c), (1 - e, c), (1 - e, 1 - c)]
    core_peer = (l, d, tensor_of(e, 1 - c))
    y_peers = [(l, ((y + k) % ny) * 2 + xh, t) for k in range(1, ny)]
    x_peers = [
        (l, 2 * y + 1 - xh, t),
        (l, d, tensor_of(1 - e, c)),
        (l, 2 * y + 1 - xh, tensor_of(1 - e, c)),
    ]
    above = ((l + 1) % n, d, t)
    below = ((l + n - 1) % n, d, t)
    mirror = [(last - l, d, tensor_of(k, c)) for k in range(2)]

    def send(src, dst, ssem_, rsem_, device):
        pltpu.make_async_remote_copy(
            src_ref=src, dst_ref=dst, send_sem=ssem_, recv_sem=rsem_,
            device_id=device, device_id_type=MESH,
        ).start()

    def wait_for(ref, sem):
        pltpu.make_async_copy(ref, ref, sem).wait()

    own_rows = pl.ds(pl.multiple_of(d * rows, rows), rows)
    pair_rows = pl.ds(pl.multiple_of(xh * rows, rows), rows)
    own_cols = pl.ds(pl.multiple_of(e * quarter, quarter), quarter)
    query_cols = pl.ds(pl.multiple_of(t * quarter, quarter), quarter)

    local = [
        pltpu.make_async_copy(wd_hbm, wd.at[own_rows], loc.at[0]),
        pltpu.make_async_copy(wo_hbm, ring.at[l], loc.at[1]),
        pltpu.make_async_copy(wq_hbm, wq.at[y, pair_rows, query_cols], loc.at[2]),
        pltpu.make_async_copy(x_hbm, xv, loc.at[3]),
    ]
    for copy in local:
        copy.start()

    barrier = pltpu.get_barrier_semaphore()

    def greet(device):
        pl.semaphore_signal(barrier, inc=1, device_id=device, device_id_type=MESH)

    greeted = gather_peers + [(l, d, tensor_of(*p)) for p in cut_peers]
    greeted += [x_peers[2], above, below] + mirror
    for device in greeted:
        greet(device)

    @pl.when(l == last)
    def _():
        def one(p, carry):
            greet((p, d, tensor_of(0, c)))
            greet((p, d, tensor_of(1, c)))
            return carry
        lax.fori_loop(0, last, one, 0)

    @pl.when(l < last)
    def _():
        greet((last, d, tensor_of(0, c)))
        greet((last, d, tensor_of(1, c)))

    pl.semaphore_wait(barrier, len(greeted) + jnp.where(l == last, 2 * last, 2))

    for copy in local:
        copy.wait()

    for device in gather_peers:
        send(wd.at[own_rows], wd.at[own_rows], asem.at[0], asem.at[1], device)

    def up_send(s):
        @pl.when((s <= l) & (l < last) & (s < up_steps))
        def _():
            j = l - s
            send(ring.at[j], ring.at[j], ups.at[s], upr.at[s], above)

    def down_valid(who, s):
        return (s < up_steps - 1) & ((who + s <= low) | (who + s >= n))

    def down_send(s):
        @pl.when(down_valid(l, s))
        def _():
            j = (l + s) % n
            send(ring.at[j], ring.at[j], dns.at[s], dnr.at[s], below)

    behind = (l + 1) % n

    def ring_step(s):
        @pl.when(s < l)
        def _():
            wait_for(ring.at[l - 1 - s], upr.at[s])
            up_send_next(s)

        @pl.when(down_valid(behind, s))
        def _():
            wait_for(ring.at[(l + 1 + s) % n], dnr.at[s])
            down_send_next(s)

    def up_send_next(s):
        @pl.when(s + 1 < up_steps)
        def _():
            up_send(s + 1)

    def down_send_next(s):
        @pl.when(s + 1 < up_steps - 1)
        def _():
            down_send(s + 1)

    up_send(0)
    down_send(0)

    def spread_first(ref, cols, s_sem, r_sem):
        for device in y_peers:
            piece = ref.at[y, pair_rows, cols]
            send(piece, piece, s_sem, r_sem, device)

    def wait_first(sem):
        if ny > 1:
            wait_for(dummy.at[pl.ds(0, ny - 1)], sem)

    def spread_second(ref, cols, s_sem, r_sem):
        for device in x_peers:
            piece = ref.at[:, pair_rows, cols]
            send(piece, piece, s_sem, r_sem, device)

    def wait_second(sem):
        wait_for(dummy, sem)

    spread_first(wq, query_cols, qsem.at[0], qsem.at[1])

    def cut_send(j, part):
        for b in range(4):
            csend[j, b] = part[:, b * quarter:(b + 1) * quarter].astype(BF16)
        for x_low, core in cut_peers:
            send(
                csend.at[j, 2 * core + x_low], crecv.at[j, t], cs.at[j], cr.at[j],
                (l, d, tensor_of(x_low, core)),
            )

    def cut_sum(j):
        wait_for(dummy.at[pl.ds(0, 3)], cr.at[j])
        crecv[j, t] = csend[j, 2 * c + e]
        total = crecv[j, 0].astype(F32)
        for k in range(1, 4):
            total = total + crecv[j, k].astype(F32)
        g[j, y, pair_rows, own_cols] = total.astype(BF16)
        spread_first(g.at[j], own_cols, d1s.at[j], d1r.at[j])

    def pass_on(j):
        wait_first(d1r.at[j])
        spread_second(g.at[j], own_cols, d2s.at[j], d2r.at[j])

    seen = jnp.sum(ring[l].astype(F32) * read_ref[...].astype(F32), axis=1, keepdims=True)
    cut_send(l, jnp.broadcast_to(seen, (rows, width)))

    early = min(3, up_steps)
    for s in range(early):
        ring_step(s)
        if s == 0:
            cut_sum(l)
            wait_first(qsem.at[1])
            spread_second(wq, query_cols, qsem.at[2], qsem.at[3])
        if s == 1:
            pass_on(l)
            wait_second(qsem.at[3])
            for k in range(2):
                cols = pl.ds(pl.multiple_of((2 * k + c) * quarter, quarter), quarter)
                piece = wq.at[:, :, cols]
                send(piece, piece, qsem.at[4], qsem.at[5], core_peer)

    i0 = lax.broadcasted_iota(jnp.int32, (seq, seq), 0)
    i1 = lax.broadcasted_iota(jnp.int32, (seq, seq), 1)
    doc0 = jnp.zeros((seq, seq), jnp.int32)
    doc1 = jnp.zeros((seq, seq), jnp.int32)
    end = jnp.int32(0)
    for k in range(len_ref.shape[1]):
        end = end + len_ref[e, k]
        doc0 = doc0 + (i0 >= end).astype(jnp.int32)
        doc1 = doc1 + (i1 >= end).astype(jnp.int32)
    maskv[...] = ((doc0 == doc1) & (i1 <= i0)).astype(F32)

    wait_for(wd.at[pl.ds(0, (nd - 1) * rows)], asem.at[1])
    head = jnp.sum(xv[...].astype(F32) * read_ref[...].astype(F32), axis=1, keepdims=True)
    for core in range(2):
        part = nt_dot(xv[...], wd[core * half:(core + 1) * half])
        for x_low in range(2):
            b = 2 * core + x_low
            p0send[b, :, 0:half] = part[x_low * seq:(x_low + 1) * seq]
            p0send[b, :, half:half + 128] = jnp.broadcast_to(
                head[x_low * seq:(x_low + 1) * seq], (seq, 128)
            )
    for x_low, core in cut_peers:
        send(
            p0send.at[2 * core + x_low], p0recv.at[t], psem.at[0], psem.at[1],
            (l, d, tensor_of(x_low, core)),
        )

    def items(s, do):
        @pl.when((s >= 0) & (s < up_steps) & (s < l))
        def _():
            do(l - 1 - s)

        @pl.when((s >= 0) & down_valid(behind, s) & ((l + 1 + s) % n < l))
        def _():
            do((l + 1 + s) % n)

    def product(j):
        cut_send(j, nt_dot(ring[j], wd[...]))

    def prepare(s, carry):
        @pl.when((s >= early) & (s < up_steps))
        def _():
            ring_step(s)
        items(s, product)
        items(s - 1, cut_sum)
        items(s - 2, pass_on)
        return carry

    lax.fori_loop(0, up_steps + 2, prepare, 0)

    @pl.when(l > 0)
    def _():
        wait_second(d2r.at[l - 1])
        send(g.at[l - 1], gnear, nx.at[0], nx.at[1], core_peer)

    wait_for(p0recv.at[pl.ds(0, 3)], psem.at[1])
    p0recv[t] = p0send[2 * c + e]
    whole = p0recv[0]
    for k in range(1, 4):
        whole = whole + p0recv[k]
    acc[...] = whole[:, 0:half]
    s0 = lax.broadcasted_iota(jnp.int32, (seq, 128), 0)
    s1 = lax.broadcasted_iota(jnp.int32, (seq, 128), 1)
    diagonal = (s0 == s1).astype(F32)

    def as_row(columns):
        row = jnp.sum(columns * diagonal, axis=0, keepdims=True)
        return jnp.broadcast_to(row, (8, 128))

    @pl.when(l == 0)
    def _():
        sin[...] = as_row(whole[:, half:half + 128])

    def mixed_in(j):
        wait_for(mixed.at[j], mr.at[j])

        @pl.when(l < last)
        def _():
            send(mixed.at[j], mixed.at[j], ms.at[j], mr.at[j], above)

    def far(j, carry):
        mixed_in(j)
        wait_second(d2r.at[j])
        acc[...] += dot(mixed[j], g[j].reshape(width, half))
        return carry

    lax.fori_loop(0, l - 1, far, 0)
    p2[c] = acc[...]
    send(p2.at[c], p2.at[c], ex.at[0], ex.at[1], core_peer)
    wait_second(d2r.at[l])
    wait_for(wq.at[:, :, pl.ds(0, half)], qsem.at[5])
    wait_for(p2.at[1 - c], ex.at[1])

    @pl.when(l == 0)
    def _():
        near2[...] = jnp.zeros_like(near2)

    @pl.when(l > 0)
    def _():
        wait_for(gnear, nx.at[1])
        mixed_in(l - 1)
        got = mixed[l - 1]
        near2[c] = dot(got, g[l - 1].reshape(width, half))
        near2[1 - c] = dot(got, gnear[...].reshape(width, half))

    part = jnp.concatenate([p2[0] + near2[0], p2[1] + near2[1]], axis=1)
    scale = lax.rsqrt(jnp.mean(part * part, axis=1, keepdims=True) + 1e-06)
    latent = (part * scale * gain_ref[...].astype(F32)).astype(BF16)
    query = dot(latent, wq[...].reshape(width, width)).astype(BF16)
    logits = nt_dot(query, latent) * (1.0 / float(width) ** 0.5)
    logits = jnp.where(maskv[...] > 0.5, logits, -1e30)
    top = jnp.max(logits, axis=1, keepdims=True)
    raised = jnp.exp(logits - top)
    weights = (raised / jnp.sum(raised, axis=1, keepdims=True)).astype(BF16)
    mixed[l] = dot(weights, latent).astype(BF16)

    @pl.when(l < last)
    def _():
        send(mixed.at[l], mixed.at[l], ms.at[l], mr.at[l], above)

    latv[...] = latent

    @pl.when(e == 0)
    def _():
        lat[0] = latent
        send(latv, lat.at[0], lats.at[0], latr.at[0], (l, d, tensor_of(1, c)))

    @pl.when(e == 1)
    def _():
        for k in range(2):
            send(latv, lat.at[1], lats.at[k], latr.at[1], mirror[k])

    value = as_row(dot(mixed[l], g[l].reshape(width, half)[:, 0:128]))

    @pl.when(l > 0)
    def _():
        wait_for(sin, ssem.at[1])

    sout[...] = sin[...] + value

    @pl.when(l < last)
    def _():
        send(sout, sin, ssem.at[0], ssem.at[1], above)
        wait_for(fin.at[0], fr.at[0])
        wait_for(fin.at[1], fr.at[1])

    @pl.when(l == last)
    def _():
        fin[e] = sout[...]
        send(sout, fin.at[e], fs.at[last], fr.at[e], (l, d, tensor_of(1 - e, c)))

        def one(p, carry):
            for k in range(2):
                send(sout, fin.at[e], fs.at[p + k * n], fr.at[e], (p, d, tensor_of(k, c)))
            return carry
        lax.fori_loop(0, last, one, 0)
        wait_for(fin.at[1 - e], fr.at[1 - e])

    @pl.when(e == 1)
    def _():
        wait_for(lat.at[0], latr.at[0])

    wait_for(lat.at[1], latr.at[1])
    lat_out[...] = lat[...]
    score_out[0:1, :] = fin[0, 0:1, 0:seq]
    score_out[1:2, :] = fin[1, 0:1, 0:seq]

    wait_for(wd.at[pl.ds(0, (nd - 1) * rows)], asem.at[0])
    wait_first(qsem.at[0])
    wait_second(qsem.at[2])
    wait_for(wq.at[:, :, pl.ds(0, half)], qsem.at[4])
    wait_for(p0recv.at[pl.ds(0, 3)], psem.at[0])
    wait_for(p2.at[c], ex.at[0])

    def ring_left(s, carry):
        @pl.when((s <= l) & (l < last))
        def _():
            wait_for(ring.at[l], ups.at[s])

        @pl.when(down_valid(l, s))
        def _():
            wait_for(ring.at[l], dns.at[s])
        return carry

    lax.fori_loop(0, up_steps, ring_left, 0)

    def item_left(j, carry):
        wait_for(dummy.at[pl.ds(0, 3)], cs.at[j])
        wait_first(d1s.at[j])
        wait_second(d2s.at[j])

        @pl.when(l < last)
        def _():
            wait_for(mixed.at[j], ms.at[j])
        return carry

    lax.fori_loop(0, l + 1, item_left, 0)

    @pl.when(l > 0)
    def _():
        wait_for(gnear, nx.at[0])

    wait_for(latv, lats.at[0])

    @pl.when(e == 1)
    def _():
        wait_for(latv, lats.at[1])

    @pl.when(l < last)
    def _():
        wait_for(sout, ssem.at[0])

    @pl.when(l == last)
    def _():
        wait_for(sout, fs.at[last])

        def one(p, carry):
            wait_for(sout, fs.at[p])
            wait_for(sout, fs.at[p + n])
            return carry
        lax.fori_loop(0, last, one, 0)


def body(inputs, lengths, w_down, w_query, w_out, gain_latent, readout):
    n = lax.axis_size("pipe")
    nd = lax.axis_size("dp")
    _, _, seq, feats = inputs.shape
    rows = w_query.shape[1]
    quarter = w_query.shape[2]
    width = rows * nd
    half = width // 2
    up_steps = n // 2
    dma = pltpu.SemaphoreType.DMA
    hbm = pl.BlockSpec(memory_space=pl.ANY)
    vmem = pl.BlockSpec(memory_space=pltpu.VMEM)
    latents, scores = pl.pallas_call(
        functools.partial(kernel, n, nd),
        out_shape=(
            jax.ShapeDtypeStruct((2, seq, width), BF16),
            jax.ShapeDtypeStruct((2, seq), F32),
        ),
        in_specs=[hbm, pl.BlockSpec(memory_space=pltpu.SMEM), hbm, hbm, hbm, vmem, vmem],
        out_specs=(vmem, vmem),
        scratch_shapes=[
            pltpu.VMEM((2 * seq, feats), BF16),
            pltpu.VMEM((width, feats), BF16),
            pltpu.VMEM((nd // 2, 2 * rows, width), BF16),
            pltpu.VMEM((n, rows, feats), BF16),
            pltpu.VMEM((n, 4, rows, quarter), BF16),
            pltpu.VMEM((n, 4, rows, quarter), BF16),
            pltpu.VMEM((n, nd // 2, 2 * rows, half), BF16),
            pltpu.VMEM((nd // 2, 2 * rows, half), BF16),
            pltpu.VMEM((4, seq, half + 128), F32),
            pltpu.VMEM((4, seq, half + 128), F32),
            pltpu.VMEM((seq, half), F32),
            pltpu.VMEM((2, seq, half), F32),
            pltpu.VMEM((2, seq, half), F32),
            pltpu.VMEM((n, seq, width), BF16),
            pltpu.VMEM((seq, width), BF16),
            pltpu.VMEM((2, seq, width), BF16),
            pltpu.VMEM((8, 128), F32),
            pltpu.VMEM((8, 128), F32),
            pltpu.VMEM((2, 8, 128), F32),
            pltpu.VMEM((seq, seq), F32),
            pltpu.VMEM((3 * max(nd // 2, 1), rows, quarter), BF16),
            dma((4,)),
            dma((2,)),
            dma((6,)),
            dma((up_steps,)),
            dma((up_steps,)),
            dma((up_steps,)),
            dma((up_steps,)),
            dma((n,)),
            dma((n,)),
            dma((n,)),
            dma((n,)),
            dma((n,)),
            dma((n,)),
            dma((2,)),
            dma((2,)),
            dma((n,)),
            dma((n,)),
            dma((2,)),
            dma((2,)),
            dma((2,)),
            dma((2,)),
            dma((2 * n,)),
            dma((2,)),
        ],
        compiler_params=pltpu.CompilerParams(
            collective_id=0, has_side_effects=True, vmem_limit_bytes=40 * 1024 * 1024
        ),
    )(
        inputs.reshape(2 * seq, feats),
        lengths.reshape(2, lengths.shape[2]),
        w_down[0].T,
        w_query[0],
        w_out[0],
        gain_latent,
        readout.reshape(1, feats),
    )
    return latents.reshape(1, 2, 1, seq, width), scores.reshape(2, 1, seq)


def solution(mesh):
    in_specs = (
        P(None, "dp", None, "tensor"),
        P(None, "dp", None),
        P("pipe", "tensor", "dp"),
        P("pipe", "dp", "tensor"),
        P("pipe", "dp", "tensor"),
        P("pipe", None),
        P("tensor"),
    )
    out_specs = (P("pipe", None, "dp", None, None), P(None, "dp", None))
    return jax.shard_map(body, mesh=mesh, in_specs=in_specs, out_specs=out_specs, check_vma=False)
```

```python
import functools

import jax
import jax.numpy as jnp
from jax import lax
from jax.experimental import pallas as pl
from jax.experimental.pallas import tpu as pltpu
from jax.sharding import PartitionSpec as P

F32 = jnp.float32
BF16 = jnp.bfloat16
MESH = pl.DeviceIdType.MESH


def nt_dot(a, b):
    return lax.dot_general(a, b, (((1,), (1,)), ((), ())), preferred_element_type=F32)


def dot(a, b):
    return jnp.dot(a, b, preferred_element_type=F32)


def kernel(
    n, nd,
    x_hbm, len_ref, wd_hbm, wq_hbm, wo_hbm, gain_ref, read_ref,
    lat_out, score_out,
    xv, wd, wq, ring, csend, crecv, g, gnear, p0send, p0recv, acc, p2, near2,
    mixed, latv, lat, sin, sout, fin, maskv, dummy,
    loc, asem, qsem, ups, upr, dns, dnr, cs, cr, d1s, d1r, d2s, d2r,
    nx, psem, ms, mc, mr, ex, ssem, lats, latr, fs, fr,
):
    seq = latv.shape[0]
    width = latv.shape[1]
    half = width // 2
    rows = wo_hbm.shape[0]
    quarter = wq_hbm.shape[1]
    ny = nd // 2
    up_steps = n // 2
    low = up_steps - 2
    last = n - 1

    l = lax.axis_index("pipe")
    d = lax.axis_index("dp")
    t = lax.axis_index("tensor")
    y, xh = d // 2, d % 2
    e, c = t // 2, t % 2

    def tensor_of(x_low, core):
        return 2 * x_low + core

    cut_peers = [(e, 1 - c), (1 - e, c), (1 - e, 1 - c)]
    core_peer = (l, d, tensor_of(e, 1 - c))
    y_peers = [(l, ((y + k) % ny) * 2 + xh, t) for k in range(1, ny)]
    x_peers = [
        (l, 2 * y + 1 - xh, t),
        (l, d, tensor_of(1 - e, c)),
        (l, 2 * y + 1 - xh, tensor_of(1 - e, c)),
    ]
    above = ((l + 1) % n, d, t)
    below = ((l + n - 1) % n, d, t)
    above_two = ((l + 2) % n, d, t)
    below_two = ((l + n - 2) % n, d, t)
    mirror = [(last - l, d, k) for k in range(4)]

    def send(src, dst, ssem_, rsem_, device):
        pltpu.make_async_remote_copy(
            src_ref=src, dst_ref=dst, send_sem=ssem_, recv_sem=rsem_,
            device_id=device, device_id_type=MESH,
        ).start()

    def wait_for(ref, sem):
        pltpu.make_async_copy(ref, ref, sem).wait()

    own_rows = pl.ds(pl.multiple_of(d * rows, rows), rows)
    pair_rows = pl.ds(pl.multiple_of(xh * rows, rows), rows)
    own_cols = pl.ds(pl.multiple_of(e * quarter, quarter), quarter)
    query_cols = pl.ds(pl.multiple_of(t * quarter, quarter), quarter)

    local = [
        pltpu.make_async_copy(wd_hbm, wd.at[own_rows], loc.at[0]),
        pltpu.make_async_copy(wo_hbm, ring.at[l], loc.at[1]),
        pltpu.make_async_copy(wq_hbm, wq.at[y, pair_rows, query_cols], loc.at[2]),
        pltpu.make_async_copy(x_hbm, xv, loc.at[3]),
    ]
    for copy in local:
        copy.start()

    barrier = pltpu.get_barrier_semaphore()

    def greet(device):
        pl.semaphore_signal(barrier, inc=1, device_id=device, device_id_type=MESH)

    greeted = x_peers + y_peers + [core_peer, (l, d, tensor_of(1 - e, 1 - c))]
    greeted += [above, below, above_two, below_two]
    for device in greeted:
        greet(device)

    greet((last - l, d, tensor_of(1, 0)))
    pl.semaphore_wait(barrier, len(greeted) + jnp.where(t == tensor_of(1, 0), 4, 0))

    for copy in local:
        copy.wait()

    far_rows = pl.ds(pl.multiple_of((2 * y + 1 - xh) * rows, rows), rows)
    y_bytes = wd.at[pl.ds(0, (ny - 1) * rows)]

    def gather_y(cols, s_sem, r_sem):
        for device in y_peers:
            send(wd.at[cols], wd.at[cols], s_sem, r_sem, device)

    send(wd.at[own_rows], wd.at[own_rows], asem.at[0], asem.at[1], x_peers[0])
    gather_y(own_rows, asem.at[2], asem.at[3])

    def up_send(s):
        @pl.when((s <= l) & (l < last) & (s < up_steps))
        def _():
            j = l - s
            send(ring.at[j], ring.at[j], ups.at[s], upr.at[s], above)

    def down_valid(who, s):
        return (s < up_steps - 1) & ((who + s <= low) | (who + s >= n))

    def down_send(s):
        @pl.when(down_valid(l, s))
        def _():
            j = (l + s) % n
            send(ring.at[j], ring.at[j], dns.at[s], dnr.at[s], below)

    behind = (l + 1) % n

    def ring_step(s):
        @pl.when(s < l)
        def _():
            wait_for(ring.at[l - 1 - s], upr.at[s])
            up_send_next(s)

        @pl.when(down_valid(behind, s))
        def _():
            wait_for(ring.at[(l + 1 + s) % n], dnr.at[s])
            down_send_next(s)

    def up_send_next(s):
        @pl.when(s + 1 < up_steps)
        def _():
            up_send(s + 1)

    def down_send_next(s):
        @pl.when(s + 1 < up_steps - 1)
        def _():
            down_send(s + 1)

    up_send(0)
    down_send(0)

    def spread_first(ref, cols, s_sem, r_sem):
        for device in x_peers:
            piece = ref.at[y, pair_rows, cols]
            send(piece, piece, s_sem, r_sem, device)

    def wait_first(sem):
        wait_for(dummy.at[pl.ds(0, 3)], sem)

    def spread_second(piece, s_sem, r_sem):
        for device in y_peers:
            send(piece, piece, s_sem, r_sem, device)

    def wait_second(sem):
        if ny > 1:
            wait_for(dummy, sem)

    spread_first(wq, query_cols, qsem.at[0], qsem.at[1])

    def cut_send(j, part):
        for b in range(4):
            csend[j, b] = part[:, b * quarter:(b + 1) * quarter].astype(BF16)
        for x_low, core in cut_peers:
            send(
                csend.at[j, 2 * core + x_low], crecv.at[j, t], cs.at[j], cr.at[j],
                (l, d, tensor_of(x_low, core)),
            )

    def cut_sum(j):
        wait_for(dummy.at[pl.ds(0, 3)], cr.at[j])
        crecv[j, t] = csend[j, 2 * c + e]
        total = crecv[j, 0].astype(F32)
        for k in range(1, 4):
            total = total + crecv[j, k].astype(F32)
        g[j, y, pair_rows, own_cols] = total.astype(BF16)
        spread_first(g.at[j], own_cols, d1s.at[j], d1r.at[j])

    def pass_on(j):
        wait_first(d1r.at[j])
        spread_second(g.at[j, y], d2s.at[j], d2r.at[j])

    seen = jnp.sum(ring[l].astype(F32) * read_ref[...].astype(F32), axis=1, keepdims=True)
    cut_send(l, jnp.broadcast_to(seen, (rows, width)))

    early = min(3, up_steps)
    for s in range(early):
        ring_step(s)
        if s == 0:
            cut_sum(l)
            wait_first(qsem.at[1])
            for k in range(2):
                cols = pl.ds(pl.multiple_of((2 * k + c) * quarter, quarter), quarter)
                spread_second(wq.at[y, :, cols], qsem.at[2], qsem.at[3])
            wait_for(wd.at[far_rows], asem.at[1])
            gather_y(far_rows, asem.at[4], asem.at[5])
        if s == 1:
            pass_on(l)
            wait_second(qsem.at[3])

            @pl.when(c == 1)
            def _():
                for k in range(2):
                    cols = pl.ds((2 * k + 1) * quarter, quarter)
                    piece = wq.at[:, :, cols]
                    send(piece, piece, qsem.at[4], qsem.at[5], core_peer)

    i0 = lax.broadcasted_iota(jnp.int32, (seq, seq), 0)
    i1 = lax.broadcasted_iota(jnp.int32, (seq, seq), 1)
    doc0 = jnp.zeros((seq, seq), jnp.int32)
    doc1 = jnp.zeros((seq, seq), jnp.int32)
    end = jnp.int32(0)
    for k in range(len_ref.shape[1]):
        end = end + len_ref[e, k]
        doc0 = doc0 + (i0 >= end).astype(jnp.int32)
        doc1 = doc1 + (i1 >= end).astype(jnp.int32)
    maskv[...] = ((doc0 == doc1) & (i1 <= i0)).astype(F32)

    if ny > 1:
        wait_for(y_bytes, asem.at[3])
        wait_for(y_bytes, asem.at[5])
    head = jnp.sum(xv[...].astype(F32) * read_ref[...].astype(F32), axis=1, keepdims=True)
    for core in range(2):
        part = nt_dot(xv[...], wd[core * half:(core + 1) * half])
        for x_low in range(2):
            b = 2 * core + x_low
            p0send[b, :, 0:half] = part[x_low * seq:(x_low + 1) * seq]
            p0send[b, :, half:half + 128] = jnp.broadcast_to(
                head[x_low * seq:(x_low + 1) * seq], (seq, 128)
            )
    for x_low, core in cut_peers:
        send(
            p0send.at[2 * core + x_low], p0recv.at[t], psem.at[0], psem.at[1],
            (l, d, tensor_of(x_low, core)),
        )

    def items(s, do):
        @pl.when((s >= 0) & (s < up_steps) & (s < l))
        def _():
            do(l - 1 - s)

        @pl.when((s >= 0) & down_valid(behind, s) & ((l + 1 + s) % n < l))
        def _():
            do((l + 1 + s) % n)

    def product(j):
        cut_send(j, nt_dot(ring[j], wd[...]))

    def prepare(s, carry):
        @pl.when((s >= early) & (s < up_steps))
        def _():
            ring_step(s)
        items(s, product)
        items(s - 1, cut_sum)
        items(s - 2, pass_on)
        return carry

    ready = jnp.minimum(l, up_steps) + 2
    lax.fori_loop(0, ready, prepare, 0)

    close = 3
    for k in range(close):
        @pl.when((l > k) & (c == 1))
        def _():
            wait_second(d2r.at[l - 1 - k])
            send(g.at[l - 1 - k], gnear.at[k], nx.at[k], nx.at[close + k], core_peer)

    wait_for(p0recv.at[pl.ds(0, 3)], psem.at[1])
    p0recv[t] = p0send[2 * c + e]
    whole = p0recv[0]
    for k in range(1, 4):
        whole = whole + p0recv[k]
    acc[...] = whole[:, 0:half]
    s0 = lax.broadcasted_iota(jnp.int32, (seq, 128), 0)
    s1 = lax.broadcasted_iota(jnp.int32, (seq, 128), 1)
    diagonal = (s0 == s1).astype(F32)

    def as_row(columns):
        row = jnp.sum(columns * diagonal, axis=0, keepdims=True)
        return jnp.broadcast_to(row, (8, 128))

    @pl.when(l == 0)
    def _():
        sin[...] = as_row(whole[:, half:half + 128])

    def add(j):
        wait_second(d2r.at[j])
        acc[...] += dot(mixed[j], g[j].reshape(width, half))

    def take(j):
        wait_for(mixed.at[j], mr.at[j])

        @pl.when(l < last)
        def _():
            send(mixed.at[j], mixed.at[j], ms.at[j], mr.at[j], above)

    def far(j, carry):
        take(j)
        send(mixed.at[j], mixed.at[j], mc.at[j], mr.at[j], core_peer)
        add(j)
        return carry

    def far_helper(j, carry):
        wait_for(mixed.at[j], mr.at[j])
        add(j)
        return carry

    def pass_down(s, carry):
        ring_step(s)
        return carry

    later = jnp.maximum(ready, early)

    @pl.when(c == 1)
    def _():
        lax.fori_loop(0, l - close, far_helper, 0)
        p2[...] = acc[...]
        send(p2, p2, ex.at[0], ex.at[1], core_peer)
        lax.fori_loop(later, up_steps, pass_down, 0)
        wait_second(d2r.at[l])

    @pl.when(c == 0)
    def _():
        lax.fori_loop(0, l - close, far, 0)
        for k in range(close - 1, 0, -1):
            @pl.when(l > k)
            def _():
                take(l - 1 - k)

        wait_for(wq.at[:, :, pl.ds(0, half)], qsem.at[5])
        wait_for(p2, ex.at[1])
        near2[0] = acc[...]
        near2[1] = p2[...]

        def near(k):
            wait_for(gnear.at[k], nx.at[close + k])
            wait_second(d2r.at[l - 1 - k])
            got = mixed[l - 1 - k]
            near2[0] += dot(got, g[l - 1 - k].reshape(width, half))
            near2[1] += dot(got, gnear[k].reshape(width, half))

        for k in range(close - 1, 0, -1):
            @pl.when(l > k)
            def _():
                near(k)

        @pl.when(l > 0)
        def _():
            wait_for(mixed.at[l - 1], mr.at[l - 1])
            near(0)

        part = jnp.concatenate([near2[0], near2[1]], axis=1)
        scale = lax.rsqrt(jnp.mean(part * part, axis=1, keepdims=True) + 1e-06)
        latent = (part * scale * gain_ref[...].astype(F32)).astype(BF16)
        query = dot(latent, wq[...].reshape(width, width)).astype(BF16)
        logits = nt_dot(query, latent) * (1.0 / float(width) ** 0.5)
        logits = jnp.where(maskv[...] > 0.5, logits, -1e30)
        top = jnp.max(logits, axis=1, keepdims=True)
        raised = jnp.exp(logits - top)
        weights = (raised / jnp.sum(raised, axis=1, keepdims=True)).astype(BF16)
        mixed[l] = dot(weights, latent).astype(BF16)

        @pl.when(l < last)
        def _():
            send(mixed.at[l], mixed.at[l], ms.at[l], mr.at[l], above)

        latv[...] = latent
        wait_second(d2r.at[l])
        value = as_row(dot(mixed[l], g[l].reshape(width, half)[:, 0:128]))

        @pl.when(l < last)
        def _():
            wait_for(mixed.at[l], ms.at[l])

        @pl.when(l + 1 < last)
        def _():
            send(mixed.at[l], mixed.at[l], ms.at[n], mr.at[l], above_two)

        @pl.when(l > 0)
        def _():
            wait_for(sin, ssem.at[1])

        sout[...] = sin[...] + value

        @pl.when(l < last)
        def _():
            send(sout, sin, ssem.at[0], ssem.at[1], above)

        @pl.when(l == last)
        def _():
            fin[e] = sout[...]
            send(sout, fin.at[e], fs.at[last], fr.at[e], (l, d, tensor_of(1 - e, 0)))

            def one(p, carry):
                for k in range(2):
                    send(
                        sout, fin.at[e], fs.at[p + k * n], fr.at[e],
                        (p, d, tensor_of(k, 0)),
                    )
                return carry
            lax.fori_loop(0, last, one, 0)

        @pl.when(e == 0)
        def _():
            lat[0] = latent
            for k in range(1, 4):
                send(latv, lat.at[0], lats.at[k], latr.at[0], (l, d, k))

        @pl.when(e == 1)
        def _():
            for k in range(4):
                send(latv, lat.at[1], lats.at[k], latr.at[1], mirror[k])

        lax.fori_loop(later, up_steps, pass_down, 0)

        @pl.when(l < last)
        def _():
            wait_for(fin.at[0], fr.at[0])
            wait_for(fin.at[1], fr.at[1])

        @pl.when(l == last)
        def _():
            wait_for(fin.at[1 - e], fr.at[1 - e])

        send(fin, fin, fs.at[2 * n - 1], fr.at[2], core_peer)

    @pl.when(c == 1)
    def _():
        wait_for(fin, fr.at[2])

    @pl.when(t > 0)
    def _():
        wait_for(lat.at[0], latr.at[0])

    wait_for(lat.at[1], latr.at[1])
    lat_out[...] = lat[...]
    score_out[0:1, :] = fin[0, 0:1, 0:seq]
    score_out[1:2, :] = fin[1, 0:1, 0:seq]

    wait_for(wd.at[own_rows], asem.at[0])
    if ny > 1:
        wait_for(y_bytes, asem.at[2])
        wait_for(y_bytes, asem.at[4])
    wait_first(qsem.at[0])
    wait_second(qsem.at[2])
    wait_for(p0recv.at[pl.ds(0, 3)], psem.at[0])

    def ring_left(s, carry):
        @pl.when((s <= l) & (l < last))
        def _():
            wait_for(ring.at[l], ups.at[s])

        @pl.when(down_valid(l, s))
        def _():
            wait_for(ring.at[l], dns.at[s])
        return carry

    lax.fori_loop(0, up_steps, ring_left, 0)

    def item_left(j, carry):
        wait_for(dummy.at[pl.ds(0, 3)], cs.at[j])
        wait_first(d1s.at[j])
        wait_second(d2s.at[j])

        @pl.when((l < last) & (j < l - 1) & (c == 0))
        def _():
            wait_for(mixed.at[j], ms.at[j])

        @pl.when((j < l - close) & (c == 0))
        def _():
            wait_for(mixed.at[j], mc.at[j])
        return carry

    lax.fori_loop(0, l + 1, item_left, 0)

    @pl.when(c == 1)
    def _():
        wait_for(wq.at[:, :, pl.ds(0, half)], qsem.at[4])
        wait_for(p2, ex.at[0])
        for k in range(close):
            @pl.when(l > k)
            def _():
                wait_for(gnear.at[k], nx.at[k])

    @pl.when(c == 0)
    def _():
        @pl.when(l + 1 < last)
        def _():
            wait_for(mixed.at[l], ms.at[n])

        for k in range(1, 4):
            wait_for(latv, lats.at[k])

        @pl.when(e == 1)
        def _():
            wait_for(latv, lats.at[0])

        @pl.when(l < last)
        def _():
            wait_for(sout, ssem.at[0])

        wait_for(fin, fs.at[2 * n - 1])

        @pl.when(l == last)
        def _():
            wait_for(sout, fs.at[last])

            def one(p, carry):
                wait_for(sout, fs.at[p])
                wait_for(sout, fs.at[p + n])
                return carry
            lax.fori_loop(0, last, one, 0)


def body(inputs, lengths, w_down, w_query, w_out, gain_latent, readout):
    n = lax.axis_size("pipe")
    nd = lax.axis_size("dp")
    _, _, seq, feats = inputs.shape
    rows = w_query.shape[1]
    quarter = w_query.shape[2]
    width = rows * nd
    half = width // 2
    up_steps = n // 2
    dma = pltpu.SemaphoreType.DMA
    hbm = pl.BlockSpec(memory_space=pl.ANY)
    vmem = pl.BlockSpec(memory_space=pltpu.VMEM)
    latents, scores = pl.pallas_call(
        functools.partial(kernel, n, nd),
        out_shape=(
            jax.ShapeDtypeStruct((2, seq, width), BF16),
            jax.ShapeDtypeStruct((2, seq), F32),
        ),
        in_specs=[hbm, pl.BlockSpec(memory_space=pltpu.SMEM), hbm, hbm, hbm, vmem, vmem],
        out_specs=(vmem, vmem),
        scratch_shapes=[
            pltpu.VMEM((2 * seq, feats), BF16),
            pltpu.VMEM((width, feats), BF16),
            pltpu.VMEM((nd // 2, 2 * rows, width), BF16),
            pltpu.VMEM((n, rows, feats), BF16),
            pltpu.VMEM((n, 4, rows, quarter), BF16),
            pltpu.VMEM((n, 4, rows, quarter), BF16),
            pltpu.VMEM((n, nd // 2, 2 * rows, half), BF16),
            pltpu.VMEM((3, nd // 2, 2 * rows, half), BF16),
            pltpu.VMEM((4, seq, half + 128), F32),
            pltpu.VMEM((4, seq, half + 128), F32),
            pltpu.VMEM((seq, half), F32),
            pltpu.VMEM((seq, half), F32),
            pltpu.VMEM((2, seq, half), F32),
            pltpu.VMEM((n, seq, width), BF16),
            pltpu.VMEM((seq, width), BF16),
            pltpu.VMEM((2, seq, width), BF16),
            pltpu.VMEM((8, 128), F32),
            pltpu.VMEM((8, 128), F32),
            pltpu.VMEM((2, 8, 128), F32),
            pltpu.VMEM((seq, seq), F32),
            pltpu.VMEM((max(4 * (nd // 2 - 1), 3), rows, quarter), BF16),
            dma((4,)),
            dma((6,)),
            dma((6,)),
            dma((up_steps,)),
            dma((up_steps,)),
            dma((up_steps,)),
            dma((up_steps,)),
            dma((n,)),
            dma((n,)),
            dma((n,)),
            dma((n,)),
            dma((n,)),
            dma((n,)),
            dma((6,)),
            dma((2,)),
            dma((n + 1,)),
            dma((n,)),
            dma((n,)),
            dma((2,)),
            dma((2,)),
            dma((4,)),
            dma((2,)),
            dma((2 * n,)),
            dma((3,)),
        ],
        compiler_params=pltpu.CompilerParams(
            collective_id=0, has_side_effects=True, vmem_limit_bytes=40 * 1024 * 1024
        ),
    )(
        inputs.reshape(2 * seq, feats),
        lengths.reshape(2, lengths.shape[2]),
        w_down[0].T,
        w_query[0],
        w_out[0],
        gain_latent,
        readout.reshape(1, feats),
    )
    return latents.reshape(1, 2, 1, seq, width), scores.reshape(2, 1, seq)


def solution(mesh):
    in_specs = (
        P(None, "dp", None, "tensor"),
        P(None, "dp", None),
        P("pipe", "tensor", "dp"),
        P("pipe", "dp", "tensor"),
        P("pipe", "dp", "tensor"),
        P("pipe", None),
        P("tensor"),
    )
    out_specs = (P("pipe", None, "dp", None, None), P(None, "dp", None))
    return jax.shard_map(body, mesh=mesh, in_specs=in_specs, out_specs=out_specs, check_vma=False)
```

```python
import functools

import jax
import jax.numpy as jnp
from jax import lax
from jax.experimental import pallas as pl
from jax.experimental.pallas import tpu as pltpu
from jax.sharding import PartitionSpec as P

F32 = jnp.float32
BF16 = jnp.bfloat16
MESH = pl.DeviceIdType.MESH


def nt_dot(a, b):
    return lax.dot_general(a, b, (((1,), (1,)), ((), ())), preferred_element_type=F32)


def dot(a, b):
    return jnp.dot(a, b, preferred_element_type=F32)


def kernel(
    n, nd,
    x_hbm, len_ref, wd_hbm, wq_hbm, wo_hbm, gain_ref, read_ref,
    lat_out, score_out,
    xv, wd, wq, ring, csend, crecv, g, gnear, p0send, p0recv, acc, p2, near2,
    mixed, latv, lat, sin, sout, fin, maskv, dummy,
    loc, asem, qsem, ups, upr, dns, dnr, cs, cr, d1s, d1r, d2s, d2r,
    nx, psem, ms, mc, mr, ex, ssem, lats, latr, fs, fr,
):
    seq = latv.shape[0]
    width = latv.shape[1]
    half = width // 2
    rows = wo_hbm.shape[0]
    quarter = wq_hbm.shape[1]
    ny = nd // 2
    up_steps = n // 2
    low = up_steps - 2
    last = n - 1

    l = lax.axis_index("pipe")
    d = lax.axis_index("dp")
    t = lax.axis_index("tensor")
    y, xh = d // 2, d % 2
    e, c = t // 2, t % 2

    def tensor_of(x_low, core):
        return 2 * x_low + core

    cut_peers = [(e, 1 - c), (1 - e, c), (1 - e, 1 - c)]
    core_peer = (l, d, tensor_of(e, 1 - c))
    y_peers = [(l, ((y + k) % ny) * 2 + xh, t) for k in range(1, ny)]
    x_peers = [
        (l, 2 * y + 1 - xh, t),
        (l, d, tensor_of(1 - e, c)),
        (l, 2 * y + 1 - xh, tensor_of(1 - e, c)),
    ]
    above = ((l + 1) % n, d, t)
    below = ((l + n - 1) % n, d, t)
    above_two = ((l + 2) % n, d, t)
    below_two = ((l + n - 2) % n, d, t)
    mirror = (last - l, d, t)

    def send(src, dst, ssem_, rsem_, device):
        pltpu.make_async_remote_copy(
            src_ref=src, dst_ref=dst, send_sem=ssem_, recv_sem=rsem_,
            device_id=device, device_id_type=MESH,
        ).start()

    def wait_for(ref, sem):
        pltpu.make_async_copy(ref, ref, sem).wait()

    own_rows = pl.ds(pl.multiple_of(d * rows, rows), rows)
    pair_rows = pl.ds(pl.multiple_of(xh * rows, rows), rows)
    own_cols = pl.ds(pl.multiple_of(e * quarter, quarter), quarter)
    query_cols = pl.ds(pl.multiple_of(t * quarter, quarter), quarter)

    local = [
        pltpu.make_async_copy(wd_hbm, wd.at[own_rows], loc.at[0]),
        pltpu.make_async_copy(wo_hbm, ring.at[l], loc.at[1]),
        pltpu.make_async_copy(wq_hbm, wq.at[y, pair_rows, query_cols], loc.at[2]),
        pltpu.make_async_copy(x_hbm, xv, loc.at[3]),
    ]
    for copy in local:
        copy.start()

    barrier = pltpu.get_barrier_semaphore()

    def greet(device):
        pl.semaphore_signal(barrier, inc=1, device_id=device, device_id_type=MESH)

    greeted = x_peers + y_peers + [core_peer, (l, d, tensor_of(1 - e, 1 - c))]
    greeted += [above, below, above_two, below_two, mirror]
    for device in greeted:
        greet(device)

    for copy in local:
        copy.wait()
    seen = jnp.sum(ring[l].astype(F32) * read_ref[...].astype(F32), axis=1, keepdims=True)
    head = jnp.sum(xv[...].astype(F32) * read_ref[...].astype(F32), axis=1, keepdims=True)
    for b in range(4):
        p0send[b, :, half:half + 128] = jnp.broadcast_to(
            head[(b % 2) * seq:(b % 2 + 1) * seq], (seq, 128)
        ).astype(BF16)
    i0 = lax.broadcasted_iota(jnp.int32, (seq, seq), 0)
    i1 = lax.broadcasted_iota(jnp.int32, (seq, seq), 1)
    doc0 = jnp.zeros((seq, seq), jnp.int32)
    doc1 = jnp.zeros((seq, seq), jnp.int32)
    end = jnp.int32(0)
    for k in range(len_ref.shape[1]):
        end = end + len_ref[e, k]
        doc0 = doc0 + (i0 >= end).astype(jnp.int32)
        doc1 = doc1 + (i1 >= end).astype(jnp.int32)
    maskv[...] = ((doc0 == doc1) & (i1 <= i0)).astype(F32)

    pl.semaphore_wait(barrier, len(greeted))

    far_rows = pl.ds(pl.multiple_of((2 * y + 1 - xh) * rows, rows), rows)
    y_bytes = wd.at[pl.ds(0, (ny - 1) * rows)]

    def gather_y(cols, s_sem, r_sem):
        for device in y_peers:
            send(wd.at[cols], wd.at[cols], s_sem, r_sem, device)

    send(wd.at[own_rows], wd.at[own_rows], asem.at[0], asem.at[1], x_peers[0])
    gather_y(own_rows, asem.at[2], asem.at[3])

    def up_send(s):
        @pl.when((s <= l) & (l < last) & (s < up_steps))
        def _():
            j = l - s
            send(ring.at[j], ring.at[j], ups.at[s], upr.at[s], above)

    def down_valid(who, s):
        return (s < up_steps - 1) & ((who + s <= low) | (who + s >= n))

    def down_send(s):
        @pl.when(down_valid(l, s))
        def _():
            j = (l + s) % n
            send(ring.at[j], ring.at[j], dns.at[s], dnr.at[s], below)

    behind = (l + 1) % n

    def ring_step(s):
        @pl.when(s < l)
        def _():
            wait_for(ring.at[l - 1 - s], upr.at[s])
            up_send_next(s)

        @pl.when(down_valid(behind, s))
        def _():
            wait_for(ring.at[(l + 1 + s) % n], dnr.at[s])
            down_send_next(s)

    def up_send_next(s):
        @pl.when(s + 1 < up_steps)
        def _():
            up_send(s + 1)

    def down_send_next(s):
        @pl.when(s + 1 < up_steps - 1)
        def _():
            down_send(s + 1)

    up_send(0)
    down_send(0)

    def spread_first(ref, cols, s_sem, r_sem):
        for device in x_peers:
            piece = ref.at[y, pair_rows, cols]
            send(piece, piece, s_sem, r_sem, device)

    def wait_first(sem):
        wait_for(dummy.at[pl.ds(0, 3)], sem)

    def spread_second(piece, s_sem, r_sem):
        for device in y_peers:
            send(piece, piece, s_sem, r_sem, device)

    def wait_second(sem):
        if ny > 1:
            wait_for(dummy, sem)

    spread_first(wq, query_cols, qsem.at[0], qsem.at[1])

    def cut_send(j, part):
        for b in range(4):
            csend[j, b] = part[:, b * quarter:(b + 1) * quarter].astype(BF16)
        for x_low, core in cut_peers:
            send(
                csend.at[j, 2 * core + x_low], crecv.at[j, t], cs.at[j], cr.at[j],
                (l, d, tensor_of(x_low, core)),
            )

    def cut_sum(j):
        wait_for(dummy.at[pl.ds(0, 3)], cr.at[j])
        crecv[j, t] = csend[j, 2 * c + e]
        total = crecv[j, 0].astype(F32)
        for k in range(1, 4):
            total = total + crecv[j, k].astype(F32)
        g[j, y, pair_rows, own_cols] = total.astype(BF16)
        spread_first(g.at[j], own_cols, d1s.at[j], d1r.at[j])

    def pass_on(j):
        wait_first(d1r.at[j])
        spread_second(g.at[j, y], d2s.at[j], d2r.at[j])

    cut_send(l, jnp.broadcast_to(seen, (rows, width)))

    early = min(3, up_steps)
    for s in range(early):
        ring_step(s)
        if s == 0:
            wait_for(wd.at[far_rows], asem.at[1])
            gather_y(far_rows, asem.at[4], asem.at[5])
            cut_sum(l)
            wait_first(qsem.at[1])
            for k in range(2):
                cols = pl.ds(pl.multiple_of((2 * k + c) * quarter, quarter), quarter)
                spread_second(wq.at[y, :, cols], qsem.at[2], qsem.at[3])
        if s == 1:
            pass_on(l)
            wait_second(qsem.at[3])

            @pl.when(c == 1)
            def _():
                for k in range(2):
                    cols = pl.ds((2 * k + 1) * quarter, quarter)
                    piece = wq.at[:, :, cols]
                    send(piece, piece, qsem.at[4], qsem.at[5], core_peer)

    if ny > 1:
        wait_for(y_bytes, asem.at[3])
        wait_for(y_bytes, asem.at[5])
    for core in range(2):
        part = nt_dot(xv[...], wd[core * half:(core + 1) * half])
        for x_low in range(2):
            b = 2 * core + x_low
            p0send[b, :, 0:half] = part[x_low * seq:(x_low + 1) * seq].astype(BF16)
    for x_low, core in cut_peers:
        send(
            p0send.at[2 * core + x_low], p0recv.at[t], psem.at[0], psem.at[1],
            (l, d, tensor_of(x_low, core)),
        )

    def items(s, do):
        @pl.when((s >= 0) & (s < up_steps) & (s < l))
        def _():
            do(l - 1 - s)

        @pl.when((s >= 0) & down_valid(behind, s) & ((l + 1 + s) % n < l))
        def _():
            do((l + 1 + s) % n)

    def product(j):
        cut_send(j, nt_dot(ring[j], wd[...]))

    def prepare(s, carry):
        @pl.when((s >= early) & (s < up_steps))
        def _():
            ring_step(s)
        items(s, product)
        items(s - 1, cut_sum)
        items(s - 2, pass_on)
        return carry

    ready = jnp.minimum(l, up_steps) + 2
    lax.fori_loop(0, ready, prepare, 0)

    close = 3
    for k in range(close):
        @pl.when((l > k) & (c == 1))
        def _():
            wait_second(d2r.at[l - 1 - k])
            send(g.at[l - 1 - k], gnear.at[k], nx.at[k], nx.at[close + k], core_peer)

    wait_for(p0recv.at[pl.ds(0, 3)], psem.at[1])
    p0recv[t] = p0send[2 * c + e]
    whole = p0recv[0].astype(F32)
    for k in range(1, 4):
        whole = whole + p0recv[k].astype(F32)
    acc[...] = whole[:, 0:half]
    s0 = lax.broadcasted_iota(jnp.int32, (seq, 128), 0)
    s1 = lax.broadcasted_iota(jnp.int32, (seq, 128), 1)
    diagonal = (s0 == s1).astype(F32)

    def as_row(columns):
        row = jnp.sum(columns * diagonal, axis=0, keepdims=True)
        return jnp.broadcast_to(row, (8, 128))

    @pl.when(l == 0)
    def _():
        sin[...] = as_row(whole[:, half:half + 128])

    def add(j):
        wait_second(d2r.at[j])
        acc[...] += dot(mixed[j], g[j].reshape(width, half))

    def take(j):
        wait_for(mixed.at[j], mr.at[j])

        @pl.when(l < last)
        def _():
            send(mixed.at[j], mixed.at[j], ms.at[j], mr.at[j], above)

    def far(j, carry):
        take(j)
        send(mixed.at[j], mixed.at[j], mc.at[j], mr.at[j], core_peer)
        add(j)
        return carry

    def far_helper(j, carry):
        wait_for(mixed.at[j], mr.at[j])
        add(j)
        return carry

    def pass_down(s, carry):
        ring_step(s)
        return carry

    later = jnp.maximum(ready, early)

    def spread_scores(core, x_low):
        def one(i, carry):
            step = (i + 1) // 2
            p = last - up_steps + jnp.where(i % 2 == 0, step, -step)
            send(fin.at[e], fin.at[e], fs.at[p], fr.at[e], (p, d, tensor_of(x_low, core)))
            return carry
        lax.fori_loop(0, last, one, 0)

    @pl.when(c == 1)
    def _():
        lax.fori_loop(0, l - close, far_helper, 0)
        p2[...] = acc[...]
        send(p2, p2, ex.at[0], ex.at[1], core_peer)
        lax.fori_loop(later, up_steps, pass_down, 0)
        wait_second(d2r.at[l])

        @pl.when(l == last)
        def _():
            wait_for(fin.at[e], fr.at[e])
            send(
                fin.at[e], fin.at[e], fs.at[last], fr.at[e], (l, d, tensor_of(1 - e, 1))
            )
            spread_scores(1, 1 - e)

    @pl.when(c == 0)
    def _():
        lax.fori_loop(0, l - close, far, 0)
        for k in range(close - 1, 0, -1):
            @pl.when(l > k)
            def _():
                take(l - 1 - k)

        wait_for(wq.at[:, :, pl.ds(0, half)], qsem.at[5])
        wait_for(p2, ex.at[1])
        near2[0] = acc[...]
        near2[1] = p2[...]

        def near(k):
            wait_for(gnear.at[k], nx.at[close + k])
            wait_second(d2r.at[l - 1 - k])
            got = mixed[l - 1 - k]
            near2[0] += dot(got, g[l - 1 - k].reshape(width, half))
            near2[1] += dot(got, gnear[k].reshape(width, half))

        for k in range(close - 1, 0, -1):
            @pl.when(l > k)
            def _():
                near(k)

        @pl.when(l > 0)
        def _():
            wait_for(mixed.at[l - 1], mr.at[l - 1])
            near(0)

        part = jnp.concatenate([near2[0], near2[1]], axis=1)
        scale = lax.rsqrt(jnp.mean(part * part, axis=1, keepdims=True) + 1e-06)
        latent = (part * scale * gain_ref[...].astype(F32)).astype(BF16)
        latv[...] = latent

        def keep():
            @pl.when(e == 0)
            def _():
                lat[0] = latv[...]
                for k in range(1, 4):
                    send(latv, lat.at[0], lats.at[k], latr.at[0], (l, d, k))

            @pl.when(e == 1)
            def _():
                send(latv, lat.at[1], lats.at[0], latr.at[1], mirror)

        @pl.when(l == last)
        def _():
            keep()

        query = dot(latent, wq[...].reshape(width, width)).astype(BF16)
        logits = nt_dot(query, latent) * (1.0 / float(width) ** 0.5)
        logits = jnp.where(maskv[...] > 0.5, logits, -1e30)
        top = jnp.max(logits, axis=1, keepdims=True)
        raised = jnp.exp(logits - top)
        weights = (raised / jnp.sum(raised, axis=1, keepdims=True)).astype(BF16)
        mixed[l] = dot(weights, latent).astype(BF16)

        @pl.when(l < last)
        def _():
            send(mixed.at[l], mixed.at[l], ms.at[l], mr.at[l], above)

        wait_second(d2r.at[l])
        value = as_row(dot(mixed[l], g[l].reshape(width, half)[:, 0:128]))

        @pl.when(l > 0)
        def _():
            wait_for(sin, ssem.at[1])

        sout[...] = sin[...] + value

        @pl.when(l < last)
        def _():
            send(sout, sin, ssem.at[0], ssem.at[1], above)

        @pl.when(l < last)
        def _():
            wait_for(mixed.at[l], ms.at[l])

        @pl.when(l + 1 < last)
        def _():
            send(mixed.at[l], mixed.at[l], ms.at[n], mr.at[l], above_two)

        @pl.when(l == last)
        def _():
            fin[e] = sout[...]
            send(fin.at[e], fin.at[e], fs.at[2 * n - 1], fr.at[e], core_peer)
            spread_scores(0, e)

        @pl.when(l < last)
        def _():
            keep()

        lax.fori_loop(later, up_steps, pass_down, 0)

    @pl.when(t == tensor_of(1, 0))
    def _():
        wait_for(lat.at[1], latr.at[1])
        for i, k in enumerate((0, 1, 3)):
            send(lat.at[1], lat.at[1], lats.at[1 + i], latr.at[1], (l, d, k))

    wait_for(wd.at[own_rows], asem.at[0])
    if ny > 1:
        wait_for(y_bytes, asem.at[2])
        wait_for(y_bytes, asem.at[4])
    wait_first(qsem.at[0])
    wait_second(qsem.at[2])
    wait_for(p0recv.at[pl.ds(0, 3)], psem.at[0])

    def ring_left(s, carry):
        @pl.when((s <= l) & (l < last))
        def _():
            wait_for(ring.at[l], ups.at[s])

        @pl.when(down_valid(l, s))
        def _():
            wait_for(ring.at[l], dns.at[s])
        return carry

    lax.fori_loop(0, up_steps, ring_left, 0)

    def item_left(j, carry):
        wait_for(dummy.at[pl.ds(0, 3)], cs.at[j])
        wait_first(d1s.at[j])
        wait_second(d2s.at[j])

        @pl.when((l < last) & (j < l - 1) & (c == 0))
        def _():
            wait_for(mixed.at[j], ms.at[j])

        @pl.when((j < l - close) & (c == 0))
        def _():
            wait_for(mixed.at[j], mc.at[j])
        return carry

    lax.fori_loop(0, l + 1, item_left, 0)

    @pl.when(c == 1)
    def _():
        wait_for(wq.at[:, :, pl.ds(0, half)], qsem.at[4])
        wait_for(p2, ex.at[0])
        for k in range(close):
            @pl.when(l > k)
            def _():
                wait_for(gnear.at[k], nx.at[k])

    @pl.when(c == 0)
    def _():
        @pl.when(l + 1 < last)
        def _():
            wait_for(mixed.at[l], ms.at[n])

        for k in range(1, 4):
            wait_for(latv, lats.at[k])

        @pl.when(e == 1)
        def _():
            wait_for(latv, lats.at[0])

        @pl.when(l < last)
        def _():
            wait_for(sout, ssem.at[0])

    @pl.when(t > 0)
    def _():
        wait_for(lat.at[0], latr.at[0])

    @pl.when(t != tensor_of(1, 0))
    def _():
        wait_for(lat.at[1], latr.at[1])

    lat_out[...] = lat[...]

    @pl.when(c == 0)
    def _():
        @pl.when(l < last)
        def _():
            wait_for(fin.at[e], fr.at[e])
            send(fin.at[e], fin.at[e], fs.at[2 * n - 1], fr.at[e], core_peer)

        wait_for(fin.at[1 - e], fr.at[1 - e])

    @pl.when(c == 1)
    def _():
        wait_for(fin.at[1 - e], fr.at[1 - e])
        send(fin.at[1 - e], fin.at[1 - e], fs.at[2 * n - 1], fr.at[1 - e], core_peer)

        @pl.when(l < last)
        def _():
            wait_for(fin.at[e], fr.at[e])

    score_out[0:1, :] = fin[0, 0:1, 0:seq]
    score_out[1:2, :] = fin[1, 0:1, 0:seq]

    wait_for(fin.at[0], fs.at[2 * n - 1])

    @pl.when(l == last)
    def _():
        def one(p, carry):
            wait_for(fin.at[0], fs.at[p])
            return carry
        lax.fori_loop(0, last + c, one, 0)


def body(inputs, lengths, w_down, w_query, w_out, gain_latent, readout):
    n = lax.axis_size("pipe")
    nd = lax.axis_size("dp")
    _, _, seq, feats = inputs.shape
    rows = w_query.shape[1]
    quarter = w_query.shape[2]
    width = rows * nd
    half = width // 2
    up_steps = n // 2
    dma = pltpu.SemaphoreType.DMA
    hbm = pl.BlockSpec(memory_space=pl.ANY)
    vmem = pl.BlockSpec(memory_space=pltpu.VMEM)
    latents, scores = pl.pallas_call(
        functools.partial(kernel, n, nd),
        out_shape=(
            jax.ShapeDtypeStruct((2, seq, width), BF16),
            jax.ShapeDtypeStruct((2, seq), F32),
        ),
        in_specs=[hbm, pl.BlockSpec(memory_space=pltpu.SMEM), hbm, hbm, hbm, vmem, vmem],
        out_specs=(vmem, vmem),
        scratch_shapes=[
            pltpu.VMEM((2 * seq, feats), BF16),
            pltpu.VMEM((width, feats), BF16),
            pltpu.VMEM((nd // 2, 2 * rows, width), BF16),
            pltpu.VMEM((n, rows, feats), BF16),
            pltpu.VMEM((n, 4, rows, quarter), BF16),
            pltpu.VMEM((n, 4, rows, quarter), BF16),
            pltpu.VMEM((n, nd // 2, 2 * rows, half), BF16),
            pltpu.VMEM((3, nd // 2, 2 * rows, half), BF16),
            pltpu.VMEM((4, seq, half + 128), BF16),
            pltpu.VMEM((4, seq, half + 128), BF16),
            pltpu.VMEM((seq, half), F32),
            pltpu.VMEM((seq, half), F32),
            pltpu.VMEM((2, seq, half), F32),
            pltpu.VMEM((n, seq, width), BF16),
            pltpu.VMEM((seq, width), BF16),
            pltpu.VMEM((2, seq, width), BF16),
            pltpu.VMEM((8, 128), F32),
            pltpu.VMEM((8, 128), F32),
            pltpu.VMEM((2, 8, 128), F32),
            pltpu.VMEM((seq, seq), F32),
            pltpu.VMEM((max(4 * (nd // 2 - 1), 3), rows, quarter), BF16),
            dma((4,)),
            dma((6,)),
            dma((6,)),
            dma((up_steps,)),
            dma((up_steps,)),
            dma((up_steps,)),
            dma((up_steps,)),
            dma((n,)),
            dma((n,)),
            dma((n,)),
            dma((n,)),
            dma((n,)),
            dma((n,)),
            dma((6,)),
            dma((2,)),
            dma((n + 1,)),
            dma((n,)),
            dma((n,)),
            dma((2,)),
            dma((2,)),
            dma((4,)),
            dma((2,)),
            dma((2 * n,)),
            dma((3,)),
        ],
        compiler_params=pltpu.CompilerParams(
            collective_id=0, has_side_effects=True, vmem_limit_bytes=60 * 1024 * 1024
        ),
    )(
        inputs.reshape(2 * seq, feats),
        lengths.reshape(2, lengths.shape[2]),
        w_down[0].T,
        w_query[0],
        w_out[0],
        gain_latent,
        readout.reshape(1, feats),
    )
    return latents.reshape(1, 2, 1, seq, width), scores.reshape(2, 1, seq)


def solution(mesh):
    in_specs = (
        P(None, "dp", None, "tensor"),
        P(None, "dp", None),
        P("pipe", "tensor", "dp"),
        P("pipe", "dp", "tensor"),
        P("pipe", "dp", "tensor"),
        P("pipe", None),
        P("tensor"),
    )
    out_specs = (P("pipe", None, "dp", None, None), P(None, "dp", None))
    return jax.shard_map(body, mesh=mesh, in_specs=in_specs, out_specs=out_specs, check_vma=False)
```

```python
import functools

import jax
import jax.numpy as jnp
from jax import lax
from jax.experimental import pallas as pl
from jax.experimental.pallas import tpu as pltpu
from jax.sharding import PartitionSpec as P

F32 = jnp.float32
BF16 = jnp.bfloat16
MESH = pl.DeviceIdType.MESH


def nt_dot(a, b):
    return lax.dot_general(a, b, (((1,), (1,)), ((), ())), preferred_element_type=F32)


def dot(a, b):
    return jnp.dot(a, b, preferred_element_type=F32)


def kernel(
    n, nd,
    x_hbm, len_ref, wd_hbm, wq_hbm, wo_hbm, gain_ref, read_ref,
    lat_out, score_out,
    xv, wd, wq, ring, csend, crecv, g, gnear, p0send, p0recv, acc, p2, near2,
    mixed, latv, lat, sin, sout, fin, maskv, dummy,
    loc, asem, qsem, ups, upr, dns, dnr, cs, cr, d1s, d1r, d2s, d2r,
    nx, psem, ms, mc, mr, ex, ssem, lats, latr, fs, fr,
):
    seq = latv.shape[0]
    width = latv.shape[1]
    half = width // 2
    rows = wo_hbm.shape[0]
    quarter = wq_hbm.shape[1]
    ny = nd // 2
    up_steps = n // 2
    low = up_steps - 2
    last = n - 1

    l = lax.axis_index("pipe")
    d = lax.axis_index("dp")
    t = lax.axis_index("tensor")
    y, xh = d // 2, d % 2
    e, c = t // 2, t % 2

    def tensor_of(x_low, core):
        return 2 * x_low + core

    cut_peers = [(e, 1 - c), (1 - e, c), (1 - e, 1 - c)]
    core_peer = (l, d, tensor_of(e, 1 - c))
    y_peers = [(l, ((y + k) % ny) * 2 + xh, t) for k in range(1, ny)]
    x_peers = [
        (l, 2 * y + 1 - xh, t),
        (l, d, tensor_of(1 - e, c)),
        (l, 2 * y + 1 - xh, tensor_of(1 - e, c)),
    ]
    above = ((l + 1) % n, d, t)
    below = ((l + n - 1) % n, d, t)
    above_two = ((l + 2) % n, d, t)
    below_two = ((l + n - 2) % n, d, t)
    mirror = (last - l, d, t)

    def send(src, dst, ssem_, rsem_, device):
        pltpu.make_async_remote_copy(
            src_ref=src, dst_ref=dst, send_sem=ssem_, recv_sem=rsem_,
            device_id=device, device_id_type=MESH,
        ).start()

    def wait_for(ref, sem):
        pltpu.make_async_copy(ref, ref, sem).wait()

    own_rows = pl.ds(pl.multiple_of(d * rows, rows), rows)
    pair_rows = pl.ds(pl.multiple_of(xh * rows, rows), rows)
    own_cols = pl.ds(pl.multiple_of(e * quarter, quarter), quarter)
    query_cols = pl.ds(pl.multiple_of(t * quarter, quarter), quarter)

    local = [
        pltpu.make_async_copy(wd_hbm, wd.at[own_rows], loc.at[0]),
        pltpu.make_async_copy(wo_hbm, ring.at[l], loc.at[1]),
        pltpu.make_async_copy(wq_hbm, wq.at[y, pair_rows, query_cols], loc.at[2]),
        pltpu.make_async_copy(x_hbm, xv, loc.at[3]),
    ]
    for copy in local:
        copy.start()

    barrier = pltpu.get_barrier_semaphore()

    def greet(device):
        pl.semaphore_signal(barrier, inc=1, device_id=device, device_id_type=MESH)

    greeted = x_peers + y_peers + [core_peer, (l, d, tensor_of(1 - e, 1 - c))]
    greeted += [above, below, above_two, below_two, mirror]
    for device in greeted:
        greet(device)

    for copy in local:
        copy.wait()
    seen = jnp.sum(ring[l].astype(F32) * read_ref[...].astype(F32), axis=1, keepdims=True)
    head = jnp.sum(xv[...].astype(F32) * read_ref[...].astype(F32), axis=1, keepdims=True)
    for b in range(4):
        p0send[b, :, half:half + 128] = jnp.broadcast_to(
            head[(b % 2) * seq:(b % 2 + 1) * seq], (seq, 128)
        ).astype(BF16)
    i0 = lax.broadcasted_iota(jnp.int32, (seq, seq), 0)
    i1 = lax.broadcasted_iota(jnp.int32, (seq, seq), 1)
    doc0 = jnp.zeros((seq, seq), jnp.int32)
    doc1 = jnp.zeros((seq, seq), jnp.int32)
    end = jnp.int32(0)
    for k in range(len_ref.shape[1]):
        end = end + len_ref[e, k]
        doc0 = doc0 + (i0 >= end).astype(jnp.int32)
        doc1 = doc1 + (i1 >= end).astype(jnp.int32)
    maskv[...] = ((doc0 == doc1) & (i1 <= i0)).astype(F32)

    pl.semaphore_wait(barrier, len(greeted))

    far_rows = pl.ds(pl.multiple_of((2 * y + 1 - xh) * rows, rows), rows)
    facing = ((y + ny // 2) % ny) * 2
    own_facing = pl.ds(pl.multiple_of((facing + xh) * rows, rows), rows)
    far_facing = pl.ds(pl.multiple_of((facing + 1 - xh) * rows, rows), rows)
    y_near = [p for k, p in enumerate(y_peers) if k + 1 != ny // 2]
    y_facing = [p for k, p in enumerate(y_peers) if k + 1 == ny // 2]
    near_bytes = wd.at[pl.ds(0, len(y_near) * rows)]

    def shard(cols, s_sem, r_sem, devices):
        for device in devices:
            send(wd.at[cols], wd.at[cols], s_sem, r_sem, device)

    shard(own_rows, asem.at[6], asem.at[7], y_facing)
    shard(own_rows, asem.at[0], asem.at[1], x_peers[:1])
    shard(own_rows, asem.at[2], asem.at[3], y_near)

    def up_send(s):
        @pl.when((s <= l) & (l < last) & (s < up_steps))
        def _():
            j = l - s
            send(ring.at[j], ring.at[j], ups.at[s], upr.at[s], above)

    def down_valid(who, s):
        return (s < up_steps - 1) & ((who + s <= low) | (who + s >= n))

    def down_send(s):
        @pl.when(down_valid(l, s))
        def _():
            j = (l + s) % n
            send(ring.at[j], ring.at[j], dns.at[s], dnr.at[s], below)

    behind = (l + 1) % n

    def ring_step(s):
        @pl.when(s < l)
        def _():
            wait_for(ring.at[l - 1 - s], upr.at[s])
            up_send_next(s)

        @pl.when(down_valid(behind, s))
        def _():
            wait_for(ring.at[(l + 1 + s) % n], dnr.at[s])
            down_send_next(s)

    def up_send_next(s):
        @pl.when(s + 1 < up_steps)
        def _():
            up_send(s + 1)

    def down_send_next(s):
        @pl.when(s + 1 < up_steps - 1)
        def _():
            down_send(s + 1)

    up_send(0)
    down_send(0)

    def spread_first(ref, cols, s_sem, r_sem):
        for device in x_peers:
            piece = ref.at[y, pair_rows, cols]
            send(piece, piece, s_sem, r_sem, device)

    def wait_first(sem):
        wait_for(dummy.at[pl.ds(0, 3)], sem)

    def spread_second(piece, s_sem, r_sem):
        for device in y_peers:
            send(piece, piece, s_sem, r_sem, device)

    def wait_second(sem):
        if ny > 1:
            wait_for(dummy, sem)

    spread_first(wq, query_cols, qsem.at[0], qsem.at[1])

    def cut_send(j, part):
        for b in range(4):
            csend[j, b] = part[:, b * quarter:(b + 1) * quarter].astype(BF16)
        for x_low, core in cut_peers:
            send(
                csend.at[j, 2 * core + x_low], crecv.at[j, t], cs.at[j], cr.at[j],
                (l, d, tensor_of(x_low, core)),
            )

    def cut_sum(j):
        wait_for(dummy.at[pl.ds(0, 3)], cr.at[j])
        crecv[j, t] = csend[j, 2 * c + e]
        total = crecv[j, 0].astype(F32)
        for k in range(1, 4):
            total = total + crecv[j, k].astype(F32)
        g[j, y, pair_rows, own_cols] = total.astype(BF16)
        spread_first(g.at[j], own_cols, d1s.at[j], d1r.at[j])

    def pass_on(j):
        wait_first(d1r.at[j])
        spread_second(g.at[j, y], d2s.at[j], d2r.at[j])

    cut_send(l, jnp.broadcast_to(seen, (rows, width)))

    early = min(3, up_steps)
    for s in range(early):
        ring_step(s)
        if s == 0:
            if y_facing:
                wait_for(wd.at[own_facing], asem.at[7])
                shard(own_facing, asem.at[8], asem.at[9], x_peers[:1])
            wait_for(wd.at[far_rows], asem.at[1])
            shard(far_rows, asem.at[4], asem.at[5], y_near)
            cut_sum(l)
            wait_first(qsem.at[1])
            for k in range(2):
                cols = pl.ds(pl.multiple_of((2 * k + c) * quarter, quarter), quarter)
                spread_second(wq.at[y, :, cols], qsem.at[2], qsem.at[3])
        if s == 1:
            wait_second(qsem.at[3])

            @pl.when(c == 1)
            def _():
                for k in range(2):
                    cols = pl.ds((2 * k + 1) * quarter, quarter)
                    piece = wq.at[:, :, cols]
                    send(piece, piece, qsem.at[4], qsem.at[5], core_peer)

    if y_facing:
        wait_for(wd.at[far_facing], asem.at[9])
    if y_near:
        wait_for(near_bytes, asem.at[3])
        wait_for(near_bytes, asem.at[5])
    for core in range(2):
        part = nt_dot(xv[...], wd[core * half:(core + 1) * half])
        for x_low in range(2):
            b = 2 * core + x_low
            p0send[b, :, 0:half] = part[x_low * seq:(x_low + 1) * seq].astype(BF16)
    for x_low, core in cut_peers:
        send(
            p0send.at[2 * core + x_low], p0recv.at[t], psem.at[0], psem.at[1],
            (l, d, tensor_of(x_low, core)),
        )

    pass_on(l)

    def items(s, do):
        @pl.when((s >= 0) & (s < up_steps) & (s < l))
        def _():
            do(l - 1 - s)

        @pl.when((s >= 0) & down_valid(behind, s) & ((l + 1 + s) % n < l))
        def _():
            do((l + 1 + s) % n)

    def product(j):
        cut_send(j, nt_dot(ring[j], wd[...]))

    def prepare(s, carry):
        @pl.when((s >= early) & (s < up_steps))
        def _():
            ring_step(s)
        items(s, product)
        items(s - 1, cut_sum)
        items(s - 2, pass_on)
        return carry

    ready = jnp.minimum(l, up_steps) + 2
    lax.fori_loop(0, ready, prepare, 0)

    close = 3
    for k in range(close):
        @pl.when((l > k) & (c == 1))
        def _():
            wait_second(d2r.at[l - 1 - k])
            send(g.at[l - 1 - k], gnear.at[k], nx.at[k], nx.at[close + k], core_peer)

    wait_for(p0recv.at[pl.ds(0, 3)], psem.at[1])
    p0recv[t] = p0send[2 * c + e]
    whole = p0recv[0].astype(F32)
    for k in range(1, 4):
        whole = whole + p0recv[k].astype(F32)
    acc[...] = whole[:, 0:half]
    s0 = lax.broadcasted_iota(jnp.int32, (seq, 128), 0)
    s1 = lax.broadcasted_iota(jnp.int32, (seq, 128), 1)
    diagonal = (s0 == s1).astype(F32)

    def as_row(columns):
        row = jnp.sum(columns * diagonal, axis=0, keepdims=True)
        return jnp.broadcast_to(row, (8, 128))

    @pl.when(l == 0)
    def _():
        sin[...] = as_row(whole[:, half:half + 128])

    def add(j):
        wait_second(d2r.at[j])
        acc[...] += dot(mixed[j], g[j].reshape(width, half))

    def take(j):
        wait_for(mixed.at[j], mr.at[j])

        @pl.when(l < last)
        def _():
            send(mixed.at[j], mixed.at[j], ms.at[j], mr.at[j], above)

    def far(j, carry):
        take(j)
        send(mixed.at[j], mixed.at[j], mc.at[j], mr.at[j], core_peer)
        add(j)
        return carry

    def far_helper(j, carry):
        wait_for(mixed.at[j], mr.at[j])
        add(j)
        return carry

    def pass_down(s, carry):
        ring_step(s)
        return carry

    later = jnp.maximum(ready, early)

    def spread_scores(core, x_low):
        def one(i, carry):
            step = (i + 1) // 2
            p = last - up_steps + jnp.where(i % 2 == 0, step, -step)
            send(fin.at[e], fin.at[e], fs.at[p], fr.at[e], (p, d, tensor_of(x_low, core)))
            return carry
        lax.fori_loop(0, last, one, 0)

    @pl.when(c == 1)
    def _():
        lax.fori_loop(0, l - close, far_helper, 0)
        p2[...] = acc[...]
        send(p2, p2, ex.at[0], ex.at[1], core_peer)
        lax.fori_loop(later, up_steps, pass_down, 0)
        wait_second(d2r.at[l])

        @pl.when(l == last)
        def _():
            wait_for(fin.at[e], fr.at[e])
            send(
                fin.at[e], fin.at[e], fs.at[last], fr.at[e], (l, d, tensor_of(1 - e, 1))
            )
            spread_scores(1, 1 - e)

    @pl.when(c == 0)
    def _():
        lax.fori_loop(0, l - close, far, 0)
        for k in range(close - 1, 0, -1):
            @pl.when(l > k)
            def _():
                take(l - 1 - k)

        wait_for(wq.at[:, :, pl.ds(0, half)], qsem.at[5])
        wait_for(p2, ex.at[1])
        near2[0] = acc[...]
        near2[1] = p2[...]

        def near(k):
            wait_for(gnear.at[k], nx.at[close + k])
            wait_second(d2r.at[l - 1 - k])
            got = mixed[l - 1 - k]
            near2[0] += dot(got, g[l - 1 - k].reshape(width, half))
            near2[1] += dot(got, gnear[k].reshape(width, half))

        for k in range(close - 1, 0, -1):
            @pl.when(l > k)
            def _():
                near(k)

        @pl.when(l > 0)
        def _():
            wait_for(mixed.at[l - 1], mr.at[l - 1])
            near(0)

        part = jnp.concatenate([near2[0], near2[1]], axis=1)
        scale = lax.rsqrt(jnp.mean(part * part, axis=1, keepdims=True) + 1e-06)
        latent = (part * scale * gain_ref[...].astype(F32)).astype(BF16)
        latv[...] = latent

        def keep():
            @pl.when(e == 0)
            def _():
                lat[0] = latv[...]
                for k in range(1, 4):
                    send(latv, lat.at[0], lats.at[k], latr.at[0], (l, d, k))

            @pl.when(e == 1)
            def _():
                send(latv, lat.at[1], lats.at[0], latr.at[1], mirror)

        @pl.when(l == last)
        def _():
            keep()

        query = dot(latent, wq[...].reshape(width, width)).astype(BF16)
        logits = nt_dot(query, latent) * (1.0 / float(width) ** 0.5)
        logits = jnp.where(maskv[...] > 0.5, logits, -1e30)
        top = jnp.max(logits, axis=1, keepdims=True)
        raised = jnp.exp(logits - top)
        weights = (raised / jnp.sum(raised, axis=1, keepdims=True)).astype(BF16)
        mixed[l] = dot(weights, latent).astype(BF16)

        @pl.when(l < last)
        def _():
            send(mixed.at[l], mixed.at[l], ms.at[l], mr.at[l], above)

        wait_second(d2r.at[l])
        value = as_row(dot(mixed[l], g[l].reshape(width, half)[:, 0:128]))

        @pl.when(l > 0)
        def _():
            wait_for(sin, ssem.at[1])

        sout[...] = sin[...] + value

        @pl.when(l < last)
        def _():
            send(sout, sin, ssem.at[0], ssem.at[1], above)

        @pl.when(l < last)
        def _():
            wait_for(mixed.at[l], ms.at[l])

        @pl.when(l + 1 < last)
        def _():
            send(mixed.at[l], mixed.at[l], ms.at[n], mr.at[l], above_two)

        @pl.when(l == last)
        def _():
            fin[e] = sout[...]
            send(fin.at[e], fin.at[e], fs.at[2 * n - 1], fr.at[e], core_peer)
            spread_scores(0, e)

        @pl.when(l < last)
        def _():
            keep()

        lax.fori_loop(later, up_steps, pass_down, 0)

    @pl.when(t == tensor_of(1, 0))
    def _():
        wait_for(lat.at[1], latr.at[1])
        for i, k in enumerate((0, 1, 3)):
            send(lat.at[1], lat.at[1], lats.at[1 + i], latr.at[1], (l, d, k))

    wait_for(wd.at[own_rows], asem.at[0])
    if y_facing:
        wait_for(wd.at[own_rows], asem.at[6])
        wait_for(wd.at[own_facing], asem.at[8])
    if y_near:
        wait_for(near_bytes, asem.at[2])
        wait_for(near_bytes, asem.at[4])
    wait_first(qsem.at[0])
    wait_second(qsem.at[2])
    wait_for(p0recv.at[pl.ds(0, 3)], psem.at[0])

    def ring_left(s, carry):
        @pl.when((s <= l) & (l < last))
        def _():
            wait_for(ring.at[l], ups.at[s])

        @pl.when(down_valid(l, s))
        def _():
            wait_for(ring.at[l], dns.at[s])
        return carry

    lax.fori_loop(0, up_steps, ring_left, 0)

    def item_left(j, carry):
        wait_for(dummy.at[pl.ds(0, 3)], cs.at[j])
        wait_first(d1s.at[j])
        wait_second(d2s.at[j])

        @pl.when((l < last) & (j < l - 1) & (c == 0))
        def _():
            wait_for(mixed.at[j], ms.at[j])

        @pl.when((j < l - close) & (c == 0))
        def _():
            wait_for(mixed.at[j], mc.at[j])
        return carry

    lax.fori_loop(0, l + 1, item_left, 0)

    @pl.when(c == 1)
    def _():
        wait_for(wq.at[:, :, pl.ds(0, half)], qsem.at[4])
        wait_for(p2, ex.at[0])
        for k in range(close):
            @pl.when(l > k)
            def _():
                wait_for(gnear.at[k], nx.at[k])

    @pl.when(c == 0)
    def _():
        @pl.when(l + 1 < last)
        def _():
            wait_for(mixed.at[l], ms.at[n])

        for k in range(1, 4):
            wait_for(latv, lats.at[k])

        @pl.when(e == 1)
        def _():
            wait_for(latv, lats.at[0])

        @pl.when(l < last)
        def _():
            wait_for(sout, ssem.at[0])

    @pl.when(t > 0)
    def _():
        wait_for(lat.at[0], latr.at[0])

    @pl.when(t != tensor_of(1, 0))
    def _():
        wait_for(lat.at[1], latr.at[1])

    lat_out[...] = lat[...]

    @pl.when(c == 0)
    def _():
        @pl.when(l < last)
        def _():
            wait_for(fin.at[e], fr.at[e])
            send(fin.at[e], fin.at[e], fs.at[2 * n - 1], fr.at[e], core_peer)

        wait_for(fin.at[1 - e], fr.at[1 - e])

    @pl.when(c == 1)
    def _():
        wait_for(fin.at[1 - e], fr.at[1 - e])
        send(fin.at[1 - e], fin.at[1 - e], fs.at[2 * n - 1], fr.at[1 - e], core_peer)

        @pl.when(l < last)
        def _():
            wait_for(fin.at[e], fr.at[e])

    score_out[0:1, :] = fin[0, 0:1, 0:seq]
    score_out[1:2, :] = fin[1, 0:1, 0:seq]

    wait_for(fin.at[0], fs.at[2 * n - 1])

    @pl.when(l == last)
    def _():
        def one(p, carry):
            wait_for(fin.at[0], fs.at[p])
            return carry
        lax.fori_loop(0, last + c, one, 0)


def body(inputs, lengths, w_down, w_query, w_out, gain_latent, readout):
    n = lax.axis_size("pipe")
    nd = lax.axis_size("dp")
    _, _, seq, feats = inputs.shape
    rows = w_query.shape[1]
    quarter = w_query.shape[2]
    width = rows * nd
    half = width // 2
    up_steps = n // 2
    dma = pltpu.SemaphoreType.DMA
    hbm = pl.BlockSpec(memory_space=pl.ANY)
    vmem = pl.BlockSpec(memory_space=pltpu.VMEM)
    latents, scores = pl.pallas_call(
        functools.partial(kernel, n, nd),
        out_shape=(
            jax.ShapeDtypeStruct((2, seq, width), BF16),
            jax.ShapeDtypeStruct((2, seq), F32),
        ),
        in_specs=[hbm, pl.BlockSpec(memory_space=pltpu.SMEM), hbm, hbm, hbm, vmem, vmem],
        out_specs=(vmem, vmem),
        scratch_shapes=[
            pltpu.VMEM((2 * seq, feats), BF16),
            pltpu.VMEM((width, feats), BF16),
            pltpu.VMEM((nd // 2, 2 * rows, width), BF16),
            pltpu.VMEM((n, rows, feats), BF16),
            pltpu.VMEM((n, 4, rows, quarter), BF16),
            pltpu.VMEM((n, 4, rows, quarter), BF16),
            pltpu.VMEM((n, nd // 2, 2 * rows, half), BF16),
            pltpu.VMEM((3, nd // 2, 2 * rows, half), BF16),
            pltpu.VMEM((4, seq, half + 128), BF16),
            pltpu.VMEM((4, seq, half + 128), BF16),
            pltpu.VMEM((seq, half), F32),
            pltpu.VMEM((seq, half), F32),
            pltpu.VMEM((2, seq, half), F32),
            pltpu.VMEM((n, seq, width), BF16),
            pltpu.VMEM((seq, width), BF16),
            pltpu.VMEM((2, seq, width), BF16),
            pltpu.VMEM((8, 128), F32),
            pltpu.VMEM((8, 128), F32),
            pltpu.VMEM((2, 8, 128), F32),
            pltpu.VMEM((seq, seq), F32),
            pltpu.VMEM((max(4 * (nd // 2 - 1), 3), rows, quarter), BF16),
            dma((4,)),
            dma((10,)),
            dma((6,)),
            dma((up_steps,)),
            dma((up_steps,)),
            dma((up_steps,)),
            dma((up_steps,)),
            dma((n,)),
            dma((n,)),
            dma((n,)),
            dma((n,)),
            dma((n,)),
            dma((n,)),
            dma((6,)),
            dma((2,)),
            dma((n + 1,)),
            dma((n,)),
            dma((n,)),
            dma((2,)),
            dma((2,)),
            dma((4,)),
            dma((2,)),
            dma((2 * n,)),
            dma((3,)),
        ],
        compiler_params=pltpu.CompilerParams(
            collective_id=0, has_side_effects=True, vmem_limit_bytes=60 * 1024 * 1024
        ),
    )(
        inputs.reshape(2 * seq, feats),
        lengths.reshape(2, lengths.shape[2]),
        w_down[0].T,
        w_query[0],
        w_out[0],
        gain_latent,
        readout.reshape(1, feats),
    )
    return latents.reshape(1, 2, 1, seq, width), scores.reshape(2, 1, seq)


def solution(mesh):
    in_specs = (
        P(None, "dp", None, "tensor"),
        P(None, "dp", None),
        P("pipe", "tensor", "dp"),
        P("pipe", "dp", "tensor"),
        P("pipe", "dp", "tensor"),
        P("pipe", None),
        P("tensor"),
    )
    out_specs = (P("pipe", None, "dp", None, None), P(None, "dp", None))
    return jax.shard_map(body, mesh=mesh, in_specs=in_specs, out_specs=out_specs, check_vma=False)
```

```python
import functools

import jax
import jax.numpy as jnp
from jax import lax
from jax.experimental import pallas as pl
from jax.experimental.pallas import tpu as pltpu
from jax.sharding import PartitionSpec as P

F32 = jnp.float32
BF16 = jnp.bfloat16
MESH = pl.DeviceIdType.MESH


def nt_dot(a, b):
    return lax.dot_general(a, b, (((1,), (1,)), ((), ())), preferred_element_type=F32)


def dot(a, b):
    return jnp.dot(a, b, preferred_element_type=F32)


def kernel(
    n, nd,
    x_hbm, len_ref, wd_hbm, wq_hbm, wo_hbm, gain_ref, read_ref,
    lat_out, score_out,
    xv, wd, wq, ring, csend, crecv, g, gnear, p0send, p0recv, acc, p2, near2,
    mixed, latv, lat, sin, sout, fin, maskv, dummy,
    loc, asem, qsem, ups, upr, dns, dnr, cs, cr, d1s, d1r, d2s, d2r,
    nx, psem, ms, mc, mr, ex, ssem, lats, latr, fs, fr,
):
    seq = latv.shape[0]
    width = latv.shape[1]
    half = width // 2
    rows = wo_hbm.shape[0]
    quarter = wq_hbm.shape[1]
    ny = nd // 2
    up_steps = n // 2
    low = up_steps - 2
    last = n - 1

    l = lax.axis_index("pipe")
    d = lax.axis_index("dp")
    t = lax.axis_index("tensor")
    y, xh = d // 2, d % 2
    e, c = t // 2, t % 2

    def tensor_of(x_low, core):
        return 2 * x_low + core

    cut_peers = [(e, 1 - c), (1 - e, c), (1 - e, 1 - c)]
    core_peer = (l, d, tensor_of(e, 1 - c))
    y_peers = [(l, ((y + k) % ny) * 2 + xh, t) for k in range(1, ny)]
    x_peers = [
        (l, 2 * y + 1 - xh, t),
        (l, d, tensor_of(1 - e, c)),
        (l, 2 * y + 1 - xh, tensor_of(1 - e, c)),
    ]
    above = ((l + 1) % n, d, t)
    below = ((l + n - 1) % n, d, t)
    above_two = ((l + 2) % n, d, t)
    below_two = ((l + n - 2) % n, d, t)
    mirror = (last - l, d, t)

    def send(src, dst, ssem_, rsem_, device):
        pltpu.make_async_remote_copy(
            src_ref=src, dst_ref=dst, send_sem=ssem_, recv_sem=rsem_,
            device_id=device, device_id_type=MESH,
        ).start()

    def wait_for(ref, sem):
        pltpu.make_async_copy(ref, ref, sem).wait()

    own_rows = pl.ds(pl.multiple_of(d * rows, rows), rows)
    pair_rows = pl.ds(pl.multiple_of(xh * rows, rows), rows)
    own_cols = pl.ds(pl.multiple_of(e * quarter, quarter), quarter)
    query_cols = pl.ds(pl.multiple_of(t * quarter, quarter), quarter)

    local = [
        pltpu.make_async_copy(wd_hbm, wd.at[own_rows], loc.at[0]),
        pltpu.make_async_copy(wo_hbm, ring.at[l], loc.at[1]),
        pltpu.make_async_copy(wq_hbm, wq.at[y, pair_rows, query_cols], loc.at[2]),
        pltpu.make_async_copy(x_hbm, xv, loc.at[3]),
    ]
    for copy in local:
        copy.start()

    barrier = pltpu.get_barrier_semaphore()

    def greet(device):
        pl.semaphore_signal(barrier, inc=1, device_id=device, device_id_type=MESH)

    greeted = x_peers + y_peers + [core_peer, (l, d, tensor_of(1 - e, 1 - c))]
    greeted += [above, below, above_two, below_two, mirror]
    for device in greeted:
        greet(device)

    for copy in local:
        copy.wait()
    seen = jnp.sum(ring[l].astype(F32) * read_ref[...].astype(F32), axis=1, keepdims=True)
    head = jnp.sum(xv[...].astype(F32) * read_ref[...].astype(F32), axis=1, keepdims=True)
    for b in range(4):
        p0send[b, :, half:half + 128] = jnp.broadcast_to(
            head[(b % 2) * seq:(b % 2 + 1) * seq], (seq, 128)
        ).astype(BF16)
    i0 = lax.broadcasted_iota(jnp.int32, (seq, seq), 0)
    i1 = lax.broadcasted_iota(jnp.int32, (seq, seq), 1)
    doc0 = jnp.zeros((seq, seq), jnp.int32)
    doc1 = jnp.zeros((seq, seq), jnp.int32)
    end = jnp.int32(0)
    for k in range(len_ref.shape[1]):
        end = end + len_ref[e, k]
        doc0 = doc0 + (i0 >= end).astype(jnp.int32)
        doc1 = doc1 + (i1 >= end).astype(jnp.int32)
    maskv[...] = ((doc0 == doc1) & (i1 <= i0)).astype(F32)

    pl.semaphore_wait(barrier, len(greeted))

    far_rows = pl.ds(pl.multiple_of((2 * y + 1 - xh) * rows, rows), rows)
    facing = ((y + ny // 2) % ny) * 2
    own_facing = pl.ds(pl.multiple_of((facing + xh) * rows, rows), rows)
    far_facing = pl.ds(pl.multiple_of((facing + 1 - xh) * rows, rows), rows)
    y_near = [p for k, p in enumerate(y_peers) if k + 1 != ny // 2]
    y_facing = [p for k, p in enumerate(y_peers) if k + 1 == ny // 2]
    near_bytes = wd.at[pl.ds(0, len(y_near) * rows)]

    def shard(cols, s_sem, r_sem, devices):
        for device in devices:
            send(wd.at[cols], wd.at[cols], s_sem, r_sem, device)

    shard(own_rows, asem.at[6], asem.at[7], y_facing)
    shard(own_rows, asem.at[0], asem.at[1], x_peers[:1])
    shard(own_rows, asem.at[2], asem.at[3], y_near)

    def up_send(s):
        @pl.when((s <= l) & (l < last) & (s < up_steps))
        def _():
            j = l - s
            send(ring.at[j], ring.at[j], ups.at[s], upr.at[s], above)

    def down_valid(who, s):
        return (s < up_steps - 1) & ((who + s <= low) | (who + s >= n))

    def down_send(s):
        @pl.when(down_valid(l, s))
        def _():
            j = (l + s) % n
            send(ring.at[j], ring.at[j], dns.at[s], dnr.at[s], below)

    behind = (l + 1) % n

    def ring_step(s):
        @pl.when(s < l)
        def _():
            wait_for(ring.at[l - 1 - s], upr.at[s])
            up_send_next(s)

        @pl.when(down_valid(behind, s))
        def _():
            wait_for(ring.at[(l + 1 + s) % n], dnr.at[s])
            down_send_next(s)

    def up_send_next(s):
        @pl.when(s + 1 < up_steps)
        def _():
            up_send(s + 1)

    def down_send_next(s):
        @pl.when(s + 1 < up_steps - 1)
        def _():
            down_send(s + 1)

    up_send(0)
    down_send(0)

    def spread_first(ref, cols, s_sem, r_sem):
        for device in x_peers:
            piece = ref.at[y, pair_rows, cols]
            send(piece, piece, s_sem, r_sem, device)

    def wait_first(sem):
        wait_for(dummy.at[pl.ds(0, 3)], sem)

    def spread_second(piece, s_sem, r_sem):
        for device in y_peers:
            send(piece, piece, s_sem, r_sem, device)

    def wait_second(sem):
        if ny > 1:
            wait_for(dummy, sem)

    spread_first(wq, query_cols, qsem.at[0], qsem.at[1])

    def cut_send(j, part):
        for b in range(4):
            csend[j, b] = part[:, b * quarter:(b + 1) * quarter].astype(BF16)
        for x_low, core in cut_peers:
            send(
                csend.at[j, 2 * core + x_low], crecv.at[j, t], cs.at[j], cr.at[j],
                (l, d, tensor_of(x_low, core)),
            )

    def cut_sum(j):
        wait_for(dummy.at[pl.ds(0, 3)], cr.at[j])
        crecv[j, t] = csend[j, 2 * c + e]
        total = crecv[j, 0].astype(F32)
        for k in range(1, 4):
            total = total + crecv[j, k].astype(F32)
        g[j, y, pair_rows, own_cols] = total.astype(BF16)
        spread_first(g.at[j], own_cols, d1s.at[j], d1r.at[j])

    def pass_on(j):
        wait_first(d1r.at[j])
        spread_second(g.at[j, y], d2s.at[j], d2r.at[j])

    cut_send(l, jnp.broadcast_to(seen, (rows, width)))

    early = min(2, up_steps)
    for s in range(early):
        ring_step(s)
        if s == 0:
            if y_facing:
                wait_for(wd.at[own_facing], asem.at[7])
                shard(own_facing, asem.at[8], asem.at[9], x_peers[:1])
            wait_for(wd.at[far_rows], asem.at[1])
            shard(far_rows, asem.at[4], asem.at[5], y_near)
            cut_sum(l)
            wait_first(qsem.at[1])
            for k in range(2):
                cols = pl.ds(pl.multiple_of((2 * k + c) * quarter, quarter), quarter)
                spread_second(wq.at[y, :, cols], qsem.at[2], qsem.at[3])
        if s == 1:
            wait_second(qsem.at[3])

            @pl.when(c == 1)
            def _():
                for k in range(2):
                    cols = pl.ds((2 * k + 1) * quarter, quarter)
                    piece = wq.at[:, :, cols]
                    send(piece, piece, qsem.at[4], qsem.at[5], core_peer)

    if y_facing:
        wait_for(wd.at[far_facing], asem.at[9])
    if y_near:
        wait_for(near_bytes, asem.at[3])
        wait_for(near_bytes, asem.at[5])
    for core in range(2):
        part = nt_dot(xv[...], wd[core * half:(core + 1) * half])
        for x_low in range(2):
            b = 2 * core + x_low
            p0send[b, :, 0:half] = part[x_low * seq:(x_low + 1) * seq].astype(BF16)
    for x_low, core in cut_peers:
        send(
            p0send.at[2 * core + x_low], p0recv.at[t], psem.at[0], psem.at[1],
            (l, d, tensor_of(x_low, core)),
        )

    pass_on(l)

    def items(s, do):
        @pl.when((s >= 0) & (s < up_steps) & (s < l))
        def _():
            do(l - 1 - s)

        @pl.when((s >= 0) & down_valid(behind, s) & ((l + 1 + s) % n < l))
        def _():
            do((l + 1 + s) % n)

    def product(j):
        cut_send(j, nt_dot(ring[j], wd[...]))

    def prepare(s, carry):
        @pl.when((s >= early) & (s < up_steps))
        def _():
            ring_step(s)
        items(s, product)
        items(s - 1, cut_sum)
        items(s - 2, pass_on)
        return carry

    ready = jnp.minimum(l, up_steps) + 2
    lax.fori_loop(0, ready, prepare, 0)

    close = 3
    for k in range(close):
        @pl.when((l > k) & (c == 1))
        def _():
            wait_second(d2r.at[l - 1 - k])
            send(g.at[l - 1 - k], gnear.at[k], nx.at[k], nx.at[close + k], core_peer)

    wait_for(p0recv.at[pl.ds(0, 3)], psem.at[1])
    p0recv[t] = p0send[2 * c + e]
    whole = p0recv[0].astype(F32)
    for k in range(1, 4):
        whole = whole + p0recv[k].astype(F32)
    acc[...] = whole[:, 0:half]
    s0 = lax.broadcasted_iota(jnp.int32, (seq, 128), 0)
    s1 = lax.broadcasted_iota(jnp.int32, (seq, 128), 1)
    diagonal = (s0 == s1).astype(F32)

    def as_row(columns):
        row = jnp.sum(columns * diagonal, axis=0, keepdims=True)
        return jnp.broadcast_to(row, (8, 128))

    @pl.when(l == 0)
    def _():
        sin[...] = as_row(whole[:, half:half + 128])

    def add(j):
        wait_second(d2r.at[j])
        acc[...] += dot(mixed[j], g[j].reshape(width, half))

    def take(j):
        wait_for(mixed.at[j], mr.at[j])

        @pl.when(l < last)
        def _():
            send(mixed.at[j], mixed.at[j], ms.at[j], mr.at[j], above)

    def far(j, carry):
        take(j)
        send(mixed.at[j], mixed.at[j], mc.at[j], mr.at[j], core_peer)
        add(j)
        return carry

    def far_helper(j, carry):
        wait_for(mixed.at[j], mr.at[j])
        add(j)
        return carry

    def pass_down(s, carry):
        ring_step(s)
        return carry

    later = jnp.maximum(ready, early)

    def spread_scores(core, x_low):
        def one(i, carry):
            step = (i + 1) // 2
            p = last - up_steps + jnp.where(i % 2 == 0, step, -step)
            send(fin.at[e], fin.at[e], fs.at[p], fr.at[e], (p, d, tensor_of(x_low, core)))
            return carry
        lax.fori_loop(0, last, one, 0)

    @pl.when(c == 1)
    def _():
        lax.fori_loop(0, l - close, far_helper, 0)
        p2[...] = acc[...]
        send(p2, p2, ex.at[0], ex.at[1], core_peer)
        lax.fori_loop(later, up_steps, pass_down, 0)
        wait_second(d2r.at[l])

        @pl.when(l == last)
        def _():
            wait_for(fin.at[e], fr.at[e])
            send(
                fin.at[e], fin.at[e], fs.at[last], fr.at[e], (l, d, tensor_of(1 - e, 1))
            )
            spread_scores(1, 1 - e)

    @pl.when(c == 0)
    def _():
        lax.fori_loop(0, l - close, far, 0)
        for k in range(close - 1, 0, -1):
            @pl.when(l > k)
            def _():
                take(l - 1 - k)

        wait_for(wq.at[:, :, pl.ds(0, half)], qsem.at[5])
        wait_for(p2, ex.at[1])
        near2[0] = acc[...]
        near2[1] = p2[...]

        def near(k):
            wait_for(gnear.at[k], nx.at[close + k])
            wait_second(d2r.at[l - 1 - k])
            got = mixed[l - 1 - k]
            near2[0] += dot(got, g[l - 1 - k].reshape(width, half))
            near2[1] += dot(got, gnear[k].reshape(width, half))

        for k in range(close - 1, 0, -1):
            @pl.when(l > k)
            def _():
                near(k)

        @pl.when(l > 0)
        def _():
            wait_for(mixed.at[l - 1], mr.at[l - 1])
            near(0)

        part = jnp.concatenate([near2[0], near2[1]], axis=1)
        scale = lax.rsqrt(jnp.mean(part * part, axis=1, keepdims=True) + 1e-06)
        latent = (part * scale * gain_ref[...].astype(F32)).astype(BF16)
        latv[...] = latent

        def keep():
            @pl.when(e == 0)
            def _():
                lat[0] = latv[...]
                for k in range(1, 4):
                    send(latv, lat.at[0], lats.at[k], latr.at[0], (l, d, k))

            @pl.when(e == 1)
            def _():
                send(latv, lat.at[1], lats.at[0], latr.at[1], mirror)

        @pl.when(l == last)
        def _():
            keep()

        query = dot(latent, wq[...].reshape(width, width)).astype(BF16)
        logits = nt_dot(query, latent) * (1.0 / float(width) ** 0.5)
        logits = jnp.where(maskv[...] > 0.5, logits, -1e30)
        top = jnp.max(logits, axis=1, keepdims=True)
        raised = jnp.exp(logits - top)
        weights = (raised / jnp.sum(raised, axis=1, keepdims=True)).astype(BF16)
        mixed[l] = dot(weights, latent).astype(BF16)

        @pl.when(l < last)
        def _():
            send(mixed.at[l], mixed.at[l], ms.at[l], mr.at[l], above)

        wait_second(d2r.at[l])
        value = as_row(dot(mixed[l], g[l].reshape(width, half)[:, 0:128]))

        @pl.when(l > 0)
        def _():
            wait_for(sin, ssem.at[1])

        sout[...] = sin[...] + value

        @pl.when(l < last)
        def _():
            send(sout, sin, ssem.at[0], ssem.at[1], above)

        @pl.when(l < last)
        def _():
            wait_for(mixed.at[l], ms.at[l])

        @pl.when(l + 1 < last)
        def _():
            send(mixed.at[l], mixed.at[l], ms.at[n], mr.at[l], above_two)

        @pl.when(l == last)
        def _():
            fin[e] = sout[...]
            send(fin.at[e], fin.at[e], fs.at[2 * n - 1], fr.at[e], core_peer)
            spread_scores(0, e)

        @pl.when(l < last)
        def _():
            keep()

        lax.fori_loop(later, up_steps, pass_down, 0)

    @pl.when(t == tensor_of(1, 0))
    def _():
        wait_for(lat.at[1], latr.at[1])
        for i, k in enumerate((0, 1, 3)):
            send(lat.at[1], lat.at[1], lats.at[1 + i], latr.at[1], (l, d, k))

    wait_for(wd.at[own_rows], asem.at[0])
    if y_facing:
        wait_for(wd.at[own_rows], asem.at[6])
        wait_for(wd.at[own_facing], asem.at[8])
    if y_near:
        wait_for(near_bytes, asem.at[2])
        wait_for(near_bytes, asem.at[4])
    wait_first(qsem.at[0])
    wait_second(qsem.at[2])
    wait_for(p0recv.at[pl.ds(0, 3)], psem.at[0])

    def ring_left(s, carry):
        @pl.when((s <= l) & (l < last))
        def _():
            wait_for(ring.at[l], ups.at[s])

        @pl.when(down_valid(l, s))
        def _():
            wait_for(ring.at[l], dns.at[s])
        return carry

    lax.fori_loop(0, up_steps, ring_left, 0)

    def item_left(j, carry):
        wait_for(dummy.at[pl.ds(0, 3)], cs.at[j])
        wait_first(d1s.at[j])
        wait_second(d2s.at[j])

        @pl.when((l < last) & (j < l - 1) & (c == 0))
        def _():
            wait_for(mixed.at[j], ms.at[j])

        @pl.when((j < l - close) & (c == 0))
        def _():
            wait_for(mixed.at[j], mc.at[j])
        return carry

    lax.fori_loop(0, l + 1, item_left, 0)

    @pl.when(c == 1)
    def _():
        wait_for(wq.at[:, :, pl.ds(0, half)], qsem.at[4])
        wait_for(p2, ex.at[0])
        for k in range(close):
            @pl.when(l > k)
            def _():
                wait_for(gnear.at[k], nx.at[k])

    @pl.when(c == 0)
    def _():
        @pl.when(l + 1 < last)
        def _():
            wait_for(mixed.at[l], ms.at[n])

        for k in range(1, 4):
            wait_for(latv, lats.at[k])

        @pl.when(e == 1)
        def _():
            wait_for(latv, lats.at[0])

        @pl.when(l < last)
        def _():
            wait_for(sout, ssem.at[0])

    @pl.when(t > 0)
    def _():
        wait_for(lat.at[0], latr.at[0])

    @pl.when(t != tensor_of(1, 0))
    def _():
        wait_for(lat.at[1], latr.at[1])

    lat_out[...] = lat[...]

    @pl.when(c == 0)
    def _():
        @pl.when(l < last)
        def _():
            wait_for(fin.at[e], fr.at[e])
            send(fin.at[e], fin.at[e], fs.at[2 * n - 1], fr.at[e], core_peer)

        wait_for(fin.at[1 - e], fr.at[1 - e])

    @pl.when(c == 1)
    def _():
        wait_for(fin.at[1 - e], fr.at[1 - e])
        send(fin.at[1 - e], fin.at[1 - e], fs.at[2 * n - 1], fr.at[1 - e], core_peer)

        @pl.when(l < last)
        def _():
            wait_for(fin.at[e], fr.at[e])

    score_out[0:1, :] = fin[0, 0:1, 0:seq]
    score_out[1:2, :] = fin[1, 0:1, 0:seq]

    wait_for(fin.at[0], fs.at[2 * n - 1])

    @pl.when(l == last)
    def _():
        def one(p, carry):
            wait_for(fin.at[0], fs.at[p])
            return carry
        lax.fori_loop(0, last + c, one, 0)


def body(inputs, lengths, w_down, w_query, w_out, gain_latent, readout):
    n = lax.axis_size("pipe")
    nd = lax.axis_size("dp")
    _, _, seq, feats = inputs.shape
    rows = w_query.shape[1]
    quarter = w_query.shape[2]
    width = rows * nd
    half = width // 2
    up_steps = n // 2
    dma = pltpu.SemaphoreType.DMA
    hbm = pl.BlockSpec(memory_space=pl.ANY)
    vmem = pl.BlockSpec(memory_space=pltpu.VMEM)
    latents, scores = pl.pallas_call(
        functools.partial(kernel, n, nd),
        out_shape=(
            jax.ShapeDtypeStruct((2, seq, width), BF16),
            jax.ShapeDtypeStruct((2, seq), F32),
        ),
        in_specs=[hbm, pl.BlockSpec(memory_space=pltpu.SMEM), hbm, hbm, hbm, vmem, vmem],
        out_specs=(vmem, vmem),
        scratch_shapes=[
            pltpu.VMEM((2 * seq, feats), BF16),
            pltpu.VMEM((width, feats), BF16),
            pltpu.VMEM((nd // 2, 2 * rows, width), BF16),
            pltpu.VMEM((n, rows, feats), BF16),
            pltpu.VMEM((n, 4, rows, quarter), BF16),
            pltpu.VMEM((n, 4, rows, quarter), BF16),
            pltpu.VMEM((n, nd // 2, 2 * rows, half), BF16),
            pltpu.VMEM((3, nd // 2, 2 * rows, half), BF16),
            pltpu.VMEM((4, seq, half + 128), BF16),
            pltpu.VMEM((4, seq, half + 128), BF16),
            pltpu.VMEM((seq, half), F32),
            pltpu.VMEM((seq, half), F32),
            pltpu.VMEM((2, seq, half), F32),
            pltpu.VMEM((n, seq, width), BF16),
            pltpu.VMEM((seq, width), BF16),
            pltpu.VMEM((2, seq, width), BF16),
            pltpu.VMEM((8, 128), F32),
            pltpu.VMEM((8, 128), F32),
            pltpu.VMEM((2, 8, 128), F32),
            pltpu.VMEM((seq, seq), F32),
            pltpu.VMEM((max(4 * (nd // 2 - 1), 3), rows, quarter), BF16),
            dma((4,)),
            dma((10,)),
            dma((6,)),
            dma((up_steps,)),
            dma((up_steps,)),
            dma((up_steps,)),
            dma((up_steps,)),
            dma((n,)),
            dma((n,)),
            dma((n,)),
            dma((n,)),
            dma((n,)),
            dma((n,)),
            dma((6,)),
            dma((2,)),
            dma((n + 1,)),
            dma((n,)),
            dma((n,)),
            dma((2,)),
            dma((2,)),
            dma((4,)),
            dma((2,)),
            dma((2 * n,)),
            dma((3,)),
        ],
        compiler_params=pltpu.CompilerParams(
            collective_id=0, has_side_effects=True, vmem_limit_bytes=60 * 1024 * 1024
        ),
    )(
        inputs.reshape(2 * seq, feats),
        lengths.reshape(2, lengths.shape[2]),
        w_down[0].T,
        w_query[0],
        w_out[0],
        gain_latent,
        readout.reshape(1, feats),
    )
    return latents.reshape(1, 2, 1, seq, width), scores.reshape(2, 1, seq)


def solution(mesh):
    in_specs = (
        P(None, "dp", None, "tensor"),
        P(None, "dp", None),
        P("pipe", "tensor", "dp"),
        P("pipe", "dp", "tensor"),
        P("pipe", "dp", "tensor"),
        P("pipe", None),
        P("tensor"),
    )
    out_specs = (P("pipe", None, "dp", None, None), P(None, "dp", None))
    return jax.shard_map(body, mesh=mesh, in_specs=in_specs, out_specs=out_specs, check_vma=False)
```
